32 devices in a mesh: ctx: 8 (over y, x, core), tp: 4 (over z).
Axes of the slice: x: 2, y: 2, z: 4, core: 2. Of those that a mesh axis runs over, the one named last changes fastest.
Arguments:
- upstream: bfloat16 [8192, 4096], P('ctx', 'tp'), may hold values from -0.75 to 0.75
- out_weight: bfloat16 [4096, 4096], P('tp'), may hold values from -0.125 to 0.125
- inner_act: bfloat16 [8192, 4096], P('ctx', 'tp'), may hold values from -6 to 6
- head_bc: bfloat16 [8192, 4096], P('ctx', 'tp'), may hold values from -0.75 to 0.75
- log_decay: float32 [32, 8192], P('tp', 'ctx'), may hold values from -1 to 0, as said below
- states: float32 [32, 32, 64, 128], P('ctx', 'tp'), may hold values from -3 to 3
- skip: float32 [32], P('tp'), may hold values from 0.1 to 1.9
Outputs:
- grad_inner: bfloat16 [8192, 4096], P('ctx', 'tp')
- grad_bc: float32 [8192, 4096], P('ctx', 'tp')
- grad_log: float32 [32, 8192], P('tp', 'ctx')
The draws below stay inside these ranges and needn't reach their ends.
Inputs may be any that keep to these rules, and one draw needn't show every extreme that they name: `log_decay`: every entry is negative.
All inputs are finite; a program needn't handle non-finite values.
Results may differ from the reference program's by a relative error of at most 0.0049.
Values may be sent and summed in bfloat16 or wider, within the bound.
A program may use at most 128 MiB of HBM per device.

```python
import math
import jax
import jax.numpy as jnp
from jax import lax

D = 4096
HEAD_TOTAL = 32
HEAD_DIM = 128
STATE = 64
BLOCK = 256
TOK_DEV = 1024
INNER = 4096
SEQUENCE_LENGTH = 8192
BLOCKS = 32


def draw_log_decay(key, part):
    random_keys = jax.random.split(jax.random.fold_in(key, 17), 7)
    fast_cut = 4
    fast = jax.random.randint(random_keys[0], (HEAD_TOTAL,), 0, 8) < fast_cut
    fast_rate = jax.random.uniform(random_keys[1], (HEAD_TOTAL,), jnp.float32, 1.0 / 50.0, 1.0 / 30.0)
    slow_rate = jax.random.uniform(random_keys[2], (HEAD_TOTAL,), jnp.float32, 0.02, 0.1) / SEQUENCE_LENGTH
    decay_rate = jnp.where(fast, fast_rate, slow_rate)
    rough_estimate = jnp.exp(jax.random.uniform(random_keys[3], (HEAD_TOTAL, SEQUENCE_LENGTH), jnp.float32, -math.log(2.0), math.log(2.0)))
    partition_scale = jnp.exp(jax.random.uniform(random_keys[4], (HEAD_TOTAL, SEQUENCE_LENGTH // TOK_DEV), jnp.float32, -math.log(2.0), math.log(2.0)))
    partition_scale = jnp.repeat(partition_scale, TOK_DEV, axis=1)
    spots = jax.random.randint(random_keys[5], (HEAD_TOTAL, 3), 0, SEQUENCE_LENGTH)
    places = jnp.arange(SEQUENCE_LENGTH, dtype=jnp.int32)
    masked_scores = jnp.any(places[None, None, :] == spots[:, :, None], axis=1)
    decay_products = jax.random.uniform(random_keys[6], (HEAD_TOTAL, SEQUENCE_LENGTH), jnp.float32, 0.223, 0.693)
    return -(decay_rate[:, None] * rough_estimate * partition_scale + jnp.where(masked_scores, decay_products, 0.0))


def with_spikes(result, key, source, target, parts, factor):
    owner, partner = [(jnp.arange(result.shape[position]) // (result.shape[position] // parts)).reshape([-1 if axis == position else 1 for axis in range(result.ndim)]) for position in (source, target)]
    chosen = jax.random.permutation(key, parts)[partner]
    strong = (owner == chosen) | (owner == (partner + parts // 2) % parts)
    return jnp.where(strong, factor * result, result)


def block_levels(own_key, extent, cuts, smallest, top_value):
    loudness = 1.0
    for dim, shards_of in cuts:
        heights = jax.random.uniform(jax.random.fold_in(jax.random.fold_in(own_key, 6), dim), (shards_of,), jnp.float32, smallest / len(cuts), top_value / len(cuts))
        loudness = loudness * jnp.repeat(jnp.exp(heights), extent[dim] // shards_of).reshape((-1,) + (1,) * (len(extent) - 1 - dim))
    return loudness


def centred(stream_key, shape, deviation, bound, cuts=(), held_as=jnp.bfloat16):
    drawn = deviation * jax.random.normal(stream_key, shape, jnp.float32)
    if cuts:
        drawn = drawn * block_levels(stream_key, shape, cuts, -0.22, 0.18)
    return jnp.clip(drawn, -bound, bound).astype(held_as)


def noise_with(stream_key, extent, width, bound, cuts, heavy, held_as=jnp.bfloat16):
    values = width * jax.random.normal(stream_key, extent, jnp.float32)
    if cuts:
        values = values * block_levels(stream_key, extent, cuts, -0.22, 0.18)
    return jnp.clip(with_spikes(values, jax.random.fold_in(stream_key, 3), *heavy), -bound, bound).astype(held_as)


def setup_inputs(seed: int = 0) -> dict:
    streams_of = jax.random.split(jax.random.key(seed), 8)
    upstream = centred(streams_of[0], (SEQUENCE_LENGTH, D), 0.125, 0.75, ((0, 8), (1, 4)))
    out_weight = noise_with(streams_of[1], (INNER, D), D ** -0.5, 0.125, ((0, 4),), (1, 0, 4, 2.0))
    inner_act = centred(streams_of[2], (SEQUENCE_LENGTH, INNER), 1.0, 6.0, ((0, 8), (1, 4)))
    head_bc = centred(streams_of[3], (SEQUENCE_LENGTH, HEAD_TOTAL * 2 * STATE), 0.125, 0.75, ((0, 8), (1, 4)))
    log_decay = draw_log_decay(jax.random.fold_in(streams_of[7], 71), 0)
    states = centred(streams_of[5], (BLOCKS, HEAD_TOTAL, STATE, HEAD_DIM), 0.5, 3.0, ((0, 8), (1, 4)), jnp.float32)
    skip = jnp.clip(1.0 + 0.18 * jax.random.normal(streams_of[6], (HEAD_TOTAL,), jnp.float32), 0.1, 1.9)
    return dict(upstream=upstream, out_weight=out_weight, inner_act=inner_act, head_bc=head_bc, log_decay=log_decay, states=states, skip=skip)


def state_end(values, b_rows, log_rate, start_state):
    cumlog = jnp.cumsum(log_rate)
    tail_decay = jnp.exp(cumlog[-1] - cumlog)
    weighted = b_rows * tail_decay[:, None]
    return jnp.exp(cumlog[-1]) * start_state + jnp.dot(weighted.T, values, precision=lax.Precision.HIGHEST)

def block_forward(values, b_rows, c_rows, log_rate, start_state):
    cumlog = jnp.cumsum(log_rate)
    log_gap = cumlog[:, None] - cumlog[None, :]
    row_ids = lax.broadcasted_iota(jnp.int32, log_gap.shape, 0)
    col_ids = lax.broadcasted_iota(jnp.int32, log_gap.shape, 1)
    decays = jnp.where(row_ids >= col_ids, jnp.exp(jnp.minimum(log_gap, 0.0)), 0.0)
    scores = jnp.dot(c_rows, b_rows.T, precision=lax.Precision.HIGHEST) * decays
    output = jnp.dot(scores, values, precision=lax.Precision.HIGHEST)
    output = output + jnp.exp(cumlog)[:, None] * jnp.dot(c_rows, start_state, precision=lax.Precision.HIGHEST)
    return (output, state_end(values, b_rows, log_rate, start_state))

def block_gradient_pass(values, b_rows, c_rows, log_rate, start_state, out_grad, carried_state):
    unused, pullback = jax.vjp(block_forward, values, b_rows, c_rows, log_rate, start_state)
    return pullback((out_grad, carried_state))

def reference(upstream, out_weight, inner_act, head_bc, log_decay, states, skip):
    out_grad = jnp.dot(upstream, out_weight.T, preferred_element_type=jnp.float32).astype(jnp.bfloat16)
    grad_vals = out_grad.astype(jnp.float32).reshape(BLOCKS, BLOCK, HEAD_TOTAL, HEAD_DIM).transpose(2, 0, 1, 3)
    inner_vals = inner_act.astype(jnp.float32).reshape(BLOCKS, BLOCK, HEAD_TOTAL, HEAD_DIM).transpose(2, 0, 1, 3)
    bc_vals = head_bc.astype(jnp.float32).reshape(BLOCKS, BLOCK, HEAD_TOTAL, 2, STATE).transpose(2, 0, 1, 3, 4)
    b_vals = bc_vals[:, :, :, 0, :]
    c_vals = bc_vals[:, :, :, 1, :]
    log_vals = log_decay.reshape(HEAD_TOTAL, BLOCKS, BLOCK)
    start_vals = states.transpose(1, 0, 2, 3)

    def head_grads(items):
        values, b_head, c_head, log_rate, start_state, head_grad = items

        def step(carried_state, block_entries):
            input_value, input_proj_value, output_proj_value, log_decay_value, state_value, output_gradient_value = block_entries
            input_gradient, input_proj_gradient, output_proj_gradient, log_decay_gradient, state_gradient = block_gradient_pass(input_value, input_proj_value, output_proj_value, log_decay_value, state_value, output_gradient_value, carried_state)
            return (state_gradient, (input_gradient, input_proj_gradient, output_proj_gradient, log_decay_gradient))
        start = jnp.zeros((STATE, HEAD_DIM), jnp.float32)
        unused, outputs = lax.scan(step, start, (values, b_head, c_head, log_rate, start_state, head_grad), reverse=True)
        return outputs
    input_gradient, input_proj_gradient, output_proj_gradient, log_decay_gradient = lax.map(head_grads, (inner_vals, b_vals, c_vals, log_vals, start_vals, grad_vals))
    input_gradient = input_gradient + skip[:, None, None, None] * grad_vals
    grad_inner = input_gradient.transpose(1, 2, 0, 3).reshape(SEQUENCE_LENGTH, INNER).astype(jnp.bfloat16)
    grad_pair = jnp.stack([input_proj_gradient, output_proj_gradient], axis=3)
    grad_bc = grad_pair.transpose(1, 2, 0, 3, 4).reshape(SEQUENCE_LENGTH, HEAD_TOTAL * 2 * STATE)
    grad_log = log_decay_gradient.reshape(HEAD_TOTAL, SEQUENCE_LENGTH)
    return (grad_inner, grad_bc, grad_log)
```

```python
import functools

import jax
import jax.numpy as jnp
from jax import lax
from jax.experimental import pallas as pl
from jax.experimental.pallas import tpu as pltpu
from jax.sharding import PartitionSpec as P

HEAD_DIM = 128
STATE = 64
BLOCK = 256
F32 = jnp.float32
BF16 = jnp.bfloat16
ROWS = (((0,), (0,)), ((), ()))
LANES = (((1,), (1,)), ((), ()))


def cumulative(log_rows):
    earlier = lax.broadcasted_iota(jnp.int32, (BLOCK, BLOCK), 0)
    later = lax.broadcasted_iota(jnp.int32, (BLOCK, BLOCK), 1)
    upto = jnp.where(earlier <= later, 1.0, 0.0)
    rows = jnp.dot(log_rows, upto, precision=lax.Precision.HIGHEST, preferred_element_type=F32)
    return rows, rows.T


def later_terms(c_rows, dy, head_decay):
    weighted = (c_rows.astype(F32) * head_decay).astype(BF16)
    return lax.dot_general(weighted, dy, ROWS, preferred_element_type=F32)


def terms_kernel(heads, bc_ref, dy_ref, log_ref, out_ref):
    @pl.when(pl.program_id(0) == 0)
    def _():
        out_ref[...] = jnp.zeros_like(out_ref)

    rows, cols = cumulative(log_ref[...])
    decay = jnp.exp(cols)
    for h in range(heads):
        c_rows = bc_ref[:, h * 128 + STATE : (h + 1) * 128]
        dy = dy_ref[:, h * 128 : (h + 1) * 128]
        term = later_terms(c_rows, dy, decay[:, h : h + 1])
        out_ref[h] = decay[BLOCK - 1 : BLOCK, h : h + 1] * out_ref[h] + term


def block_kernel(
    heads, x_ref, bc_ref, dy_ref, log_ref, s_ref, skip_ref, in_ref, gx_ref, gbc_ref, glog_ref, h_ref
):
    @pl.when(pl.program_id(0) == 0)
    def _():
        h_ref[...] = in_ref[...]

    rows, cols = cumulative(log_ref[...])
    decay = jnp.exp(cols)
    tail = jnp.exp(cols[BLOCK - 1 : BLOCK, :] - cols)
    k_ids = lax.broadcasted_iota(jnp.int32, (BLOCK, BLOCK), 0)
    q_ids = lax.broadcasted_iota(jnp.int32, (BLOCK, BLOCK), 1)
    causal = q_ids >= k_ids
    sign = jnp.where(lax.broadcasted_iota(jnp.int32, (1, 128), 1) < STATE, -1.0, 1.0)
    lane = lax.broadcasted_iota(jnp.int32, (BLOCK, heads), 1)
    token = lax.broadcasted_iota(jnp.int32, (BLOCK, 1), 0)
    dcum = jnp.zeros((BLOCK, heads), F32)
    for h in range(heads):
        here = slice(h * 128, (h + 1) * 128)
        bc = bc_ref[:, here]
        b_rows, c_rows = bc[:, :STATE], bc[:, STATE:]
        x, dy = x_ref[:, here], dy_ref[:, here]
        carried, start = h_ref[h], s_ref[0, h]
        held, start_low = carried.astype(BF16), start.astype(BF16)
        gap = rows[h : h + 1, :] - cols[:, h : h + 1]
        gate = jnp.exp(jnp.where(causal, gap, -1e30))
        scores = lax.dot_general(b_rows, c_rows, LANES, preferred_element_type=F32) * gate
        inner = lax.dot_general(x, dy, LANES, preferred_element_type=F32) * gate
        scores, inner = scores.astype(BF16), inner.astype(BF16)
        tail_h, decay_h = tail[:, h : h + 1], decay[:, h : h + 1]
        gx = jnp.dot(scores, dy, preferred_element_type=F32)
        gx += tail_h * jnp.dot(b_rows, held, preferred_element_type=F32)
        gx += skip_ref[h] * dy.astype(F32)
        gx_ref[:, here] = gx.astype(BF16)
        gb_tail = tail_h * lax.dot_general(x, held, LANES, preferred_element_type=F32)
        gb = jnp.dot(inner, c_rows, preferred_element_type=F32) + gb_tail
        gc = lax.dot_general(inner, b_rows, ROWS, preferred_element_type=F32)
        gc += decay_h * lax.dot_general(dy, start_low, LANES, preferred_element_type=F32)
        gbc = jnp.concatenate([gb, gc], axis=1)
        gbc_ref[:, here] = gbc
        dcum_h = jnp.sum(bc.astype(F32) * gbc * sign, axis=1, keepdims=True)
        whole = decay[BLOCK - 1 : BLOCK, h : h + 1]
        at_end = whole * jnp.sum(start * carried) + jnp.sum(b_rows.astype(F32) * gb_tail)
        dcum_h = dcum_h + jnp.where(token == BLOCK - 1, at_end, 0.0)
        dcum = jnp.where(lane == h, dcum_h, dcum)
        h_ref[h] = whole * carried + later_terms(c_rows, dy, decay_h)
    from_here = jnp.where(k_ids >= q_ids, 1.0, 0.0)
    glog_ref[...] = jnp.dot(
        dcum.T, from_here, precision=lax.Precision.HIGHEST, preferred_element_type=F32
    )


def later_state(part, part_log, axis):
    count, place = lax.axis_size(axis), lax.axis_index(axis)
    parts = lax.all_gather(part, axis)
    logs = lax.all_gather(part_log, axis)
    ids = jnp.arange(count)[:, None]
    between = jnp.where(ids > place, logs, 0.0)
    before = jnp.cumsum(between, axis=0) - between
    weights = jnp.where(ids > place, jnp.exp(before), 0.0)
    return jnp.sum(weights[:, :, None, None] * parts, axis=0)


def per_device(upstream, out_weight, inner_act, head_bc, log_decay, states, skip):
    tokens, heads = inner_act.shape[0], log_decay.shape[0]
    width = heads * HEAD_DIM
    blocks = tokens // BLOCK
    out_grad = lax.dot_general(
        lax.all_gather(upstream, "tp", axis=1, tiled=True),
        out_weight,
        LANES,
        preferred_element_type=F32,
    ).astype(BF16)
    wide = pl.BlockSpec((BLOCK, width), lambda i: (blocks - 1 - i, 0))
    logs = pl.BlockSpec((heads, BLOCK), lambda i: (0, blocks - 1 - i))
    carry = pl.BlockSpec((heads, STATE, HEAD_DIM), lambda i: (0, 0, 0))
    params = pltpu.CompilerParams(
        dimension_semantics=("arbitrary",), vmem_limit_bytes=48 * 1024 * 1024
    )
    part = pl.pallas_call(
        functools.partial(terms_kernel, heads),
        out_shape=jax.ShapeDtypeStruct((heads, STATE, HEAD_DIM), F32),
        grid=(blocks,),
        in_specs=[wide, wide, logs],
        out_specs=carry,
        compiler_params=params,
        name="part_terms",
    )(head_bc, out_grad, log_decay)
    incoming = later_state(part, jnp.sum(log_decay, axis=1), "ctx")
    return pl.pallas_call(
        functools.partial(block_kernel, heads),
        out_shape=(
            jax.ShapeDtypeStruct((tokens, width), BF16),
            jax.ShapeDtypeStruct((tokens, width), F32),
            jax.ShapeDtypeStruct((heads, tokens), F32),
        ),
        grid=(blocks,),
        in_specs=[
            wide,
            wide,
            wide,
            logs,
            pl.BlockSpec((1, heads, STATE, HEAD_DIM), lambda i: (blocks - 1 - i, 0, 0, 0)),
            pl.BlockSpec(memory_space=pltpu.SMEM),
            carry,
        ],
        out_specs=(wide, wide, logs),
        scratch_shapes=[pltpu.VMEM((heads, STATE, HEAD_DIM), F32)],
        compiler_params=params,
        name="block_gradients",
    )(inner_act, head_bc, out_grad, log_decay, states, skip, incoming)


def solution(mesh):
    return jax.shard_map(
        per_device,
        mesh=mesh,
        in_specs=(
            P("ctx", "tp"),
            P("tp", None),
            P("ctx", "tp"),
            P("ctx", "tp"),
            P("tp", "ctx"),
            P("ctx", "tp", None, None),
            P("tp"),
        ),
        out_specs=(P("ctx", "tp"), P("ctx", "tp"), P("tp", "ctx")),
        check_vma=False,
    )
```

```python
import functools

import jax
import jax.numpy as jnp
from jax import lax
from jax.experimental import pallas as pl
from jax.experimental.pallas import tpu as pltpu
from jax.sharding import PartitionSpec as P

HEAD_DIM = 128
STATE = 64
BLOCK = 256
CHUNK = 128
F32 = jnp.float32
BF16 = jnp.bfloat16
ROWS = (((0,), (0,)), ((), ()))
LANES = (((1,), (1,)), ((), ()))


def cumulative(log_rows):
    earlier = lax.broadcasted_iota(jnp.int32, (BLOCK, BLOCK), 0)
    later = lax.broadcasted_iota(jnp.int32, (BLOCK, BLOCK), 1)
    upto = jnp.where(earlier <= later, 1.0, 0.0)
    rows = jnp.dot(log_rows, upto, precision=lax.Precision.HIGHEST, preferred_element_type=F32)
    return rows, rows.T


def later_terms(c_rows, dy, head_decay):
    weighted = (c_rows.astype(F32) * head_decay).astype(BF16)
    return lax.dot_general(weighted, dy, ROWS, preferred_element_type=F32)


def part_combined(first, second):
    first_decay = first[STATE : STATE + 1]
    terms = first[:STATE] + first_decay * second[:STATE]
    return jnp.concatenate([terms, first[STATE:] * second[STATE:]], axis=0)


def project_kernel(
    tp,
    ctx,
    up_hbm,
    w_hbm,
    bc_hbm,
    log_ref,
    dy_ref,
    in_ref,
    got,
    w_ref,
    bc_ref,
    far_w,
    acc,
    sum_out,
    sum_in,
    weighted,
    part,
    sib_part,
    message,
    later,
    half_in,
    sib_half,
    local_sem,
    own_sem,
    relay_sem,
    got_sem,
    sum_send,
    sum_recv,
    piece_sem,
    peer_sem,
    pair_sem,
    far_sem,
    swap_sem,
    chip_send,
    chip_recv,
):
    z, me = lax.axis_index("tp"), lax.axis_index("ctx")
    core, chip = lax.rem(me, 2), lax.div(me, 2)
    sibling = me + 1 - 2 * core
    chips = ctx // 2
    heads = log_ref.shape[0]
    half = heads // 2
    tokens, depth = up_hbm.shape
    width = w_hbm.shape[0]
    piece = width // ctx
    count = tokens // CHUNK
    paired = tp == 4
    has_left, has_right = z > 0, z < tp - 1
    inner = jnp.logical_and(has_left, has_right)
    outer = jnp.logical_not(inner)

    def rows_of(c):
        return pl.ds(pl.multiple_of(c * CHUNK, CHUNK), CHUNK)

    def remote(src, dst, send, recv, **place):
        return pltpu.make_async_remote_copy(
            src_ref=src,
            dst_ref=dst,
            send_sem=send,
            recv_sem=recv,
            device_id=place,
            device_id_type=pl.DeviceIdType.MESH,
        )

    def own_copy(c, side):
        target = z - 1 if side == 0 else z + 1
        return remote(
            up_hbm.at[rows_of(c)], got.at[z, rows_of(c)], own_sem.at[side, c], got_sem.at[z, c], tp=target
        )

    def relay(s, c, target):
        place = got.at[s, rows_of(c)]
        return remote(place, place, relay_sem.at[s, c], got_sem.at[s, c], tp=target)

    def each(n, body):
        lax.fori_loop(0, n, lambda c, unused: (body(c), unused)[1], 0)

    def term(s, c):
        columns = pl.ds(pl.multiple_of(s * depth, depth), depth)
        return lax.dot_general(got[s, rows_of(c)], w_ref[:, columns], LANES, preferred_element_type=F32)

    load_w = pltpu.make_async_copy(w_hbm, w_ref, local_sem.at[0])
    load_up = pltpu.make_async_copy(up_hbm, got.at[z], local_sem.at[1])
    load_bc = pltpu.make_async_copy(bc_hbm, bc_ref, local_sem.at[2])
    load_up.start()
    load_w.start()
    load_bc.start()

    barrier = pltpu.get_barrier_semaphore()

    def greet(**place):
        pl.semaphore_signal(barrier, inc=1, device_id=place, device_id_type=pl.DeviceIdType.MESH)

    pl.when(has_left)(lambda: greet(tp=z - 1))
    pl.when(has_right)(lambda: greet(tp=z + 1))
    greet(ctx=sibling)
    for q in range(chips):
        pl.when(q != chip)(functools.partial(greet, ctx=2 * q + core))
    pl.semaphore_wait(barrier, chips + has_left.astype(jnp.int32) + has_right.astype(jnp.int32))

    low = jnp.where(z <= 1, 2, 0)

    def piece_place(j):
        return far_w.at[pl.ds(pl.multiple_of(j * piece, piece), piece)]

    def piece_down():
        source = w_hbm.at[
            pl.ds(pl.multiple_of(me * piece, piece), piece),
            pl.ds(pl.multiple_of(low * depth, depth), 2 * depth),
        ]
        return remote(source, piece_place(me), piece_sem, far_sem.at[me], tp=jnp.where(z == 0, 1, tp - 2))

    def piece_peer(q):
        place = piece_place(me)
        return remote(place, place, peer_sem.at[q], far_sem.at[me], ctx=2 * q + core)

    def piece_pair(q):
        place = piece_place(2 * q + core)
        return remote(place, place, pair_sem.at[q], far_sem.at[2 * q + core], ctx=sibling)

    def piece_wait(j):
        remote(piece_place(j), piece_place(j), piece_sem, far_sem.at[j], ctx=sibling).wait_recv()

    if paired:
        pl.when(outer)(lambda: piece_down().start())

    def send_own(c):
        pl.when(has_left)(lambda: own_copy(c, 0).start())
        pl.when(has_right)(lambda: own_copy(c, 1).start())

    each(count, send_own)
    load_up.wait()
    load_w.wait()

    def own_term(c):
        acc[rows_of(c)] = term(z, c)

    each(count, own_term)

    if paired:

        @pl.when(inner)
        def _():
            piece_wait(me)
            for q in range(chips):
                pl.when(q != chip)(lambda q=q: piece_peer(q).start())
            piece_pair(chip).start()

    load_bc.wait()
    earlier = lax.broadcasted_iota(jnp.int32, (CHUNK, CHUNK), 0)
    upto = jnp.where(earlier <= lax.broadcasted_iota(jnp.int32, (CHUNK, CHUNK), 1), 1.0, 0.0)

    def weigh(c, before):
        logs = log_ref[:, rows_of(c)]
        cumlog = before + jnp.dot(
            logs, upto, precision=lax.Precision.HIGHEST, preferred_element_type=F32
        )
        decay = jnp.exp(cumlog)
        for h in range(heads):
            c_rows = bc_ref[rows_of(c), h * 128 : (h + 1) * 128].astype(F32).T[STATE:]
            weighted[h * STATE : (h + 1) * STATE, rows_of(c)] = (c_rows * decay[h : h + 1]).astype(BF16)
        return cumlog[:, CHUNK - 1 : CHUNK]

    part_decay = jnp.exp(lax.fori_loop(0, count, weigh, jnp.zeros((heads, 1), F32)))
    for h in range(heads):
        part[h, :STATE] = jnp.zeros((STATE, HEAD_DIM), F32)
        part[h, STATE:] = jnp.broadcast_to(part_decay[h : h + 1], (8, HEAD_DIM))

    def finish(c, total):
        low_total = total.astype(BF16)
        dy_ref[rows_of(c)] = low_total
        for h in range(heads):
            part[h, :STATE] += jnp.dot(
                weighted[h * STATE : (h + 1) * STATE, rows_of(c)],
                low_total[:, h * 128 : (h + 1) * 128],
                preferred_element_type=F32,
            )

    if paired:
        end = jnp.where(z == 1, 0, 3)
        mate, far = 3 - z, 3 - end
        next_in = jnp.where(z == 0, 1, tp - 2)

        def sum_copy(c):
            return remote(
                sum_out.at[rows_of(c)], sum_in.at[rows_of(c)], sum_send.at[c], sum_recv.at[c], tp=end
            )

        def first_hop(c):
            relay(end, c, mate).wait_recv()
            relay(end, c, mate).start()
            relay(mate, c, mate).wait_recv()
            acc[rows_of(c)] += term(end, c) + term(mate, c)

        def second_hop(c):
            relay(far, c, mate).wait_recv()
            outward = lax.dot_general(
                got[low, rows_of(c)], far_w[:, :depth], LANES, preferred_element_type=F32
            )
            outward += lax.dot_general(
                got[low + 1, rows_of(c)], far_w[:, depth:], LANES, preferred_element_type=F32
            )
            sum_out[rows_of(c)] = outward.astype(BF16)
            sum_copy(c).start()
            finish(c, acc[rows_of(c)] + term(far, c))

        @pl.when(inner)
        def _():
            each(count // 2, first_hop)
            for q in range(chips):

                @pl.when(q != chip)
                def _():
                    piece_wait(2 * q + core)
                    piece_pair(q).start()

            each(count - count // 2, lambda c: first_hop(c + count // 2))
            for q in range(chips):
                piece_wait(2 * q + 1 - core)
            each(count, second_hop)

        def one_hop(c):
            relay(next_in, c, next_in).wait_recv()
            acc[rows_of(c)] += term(next_in, c)

        def last_sum(c):
            sum_copy(c).wait_recv()
            finish(c, acc[rows_of(c)] + sum_in[rows_of(c)].astype(F32))

        @pl.when(outer)
        def _():
            each(count, one_hop)
            each(count, last_sum)

    else:
        for d in range(1, tp):

            def hop(c):
                @pl.when(z >= d)
                def _():
                    relay(z - d, c, z + 1).wait_recv()
                    pl.when(has_right)(lambda: relay(z - d, c, z + 1).start())
                    acc[rows_of(c)] += term(z - d, c)

                @pl.when(z + d < tp)
                def _():
                    relay(z + d, c, z - 1).wait_recv()
                    pl.when(has_left)(lambda: relay(z + d, c, z - 1).start())
                    acc[rows_of(c)] += term(z + d, c)

            each(count, hop)
        each(count, lambda c: finish(c, acc[rows_of(c)]))

    swap = remote(part, sib_part, swap_sem.at[0], swap_sem.at[1], ctx=sibling)
    swap.start()
    swap.wait_recv()
    for j in range(half):
        mine, other = part[core * half + j], sib_part[core * half + j]
        first, second = jnp.where(core == 0, mine, other), jnp.where(core == 0, other, mine)
        message[j] = part_combined(first, second)

    def chip_copy(q):
        return remote(message, later.at[chip], chip_send.at[q], chip_recv.at[chip], ctx=2 * q + core)

    for q in reversed(range(chips)):
        pl.when(q < chip)(lambda q=q: chip_copy(q).start())
    half_in[...] = jnp.zeros_like(half_in)
    for q in reversed(range(chips)):

        @pl.when(q > chip)
        def _():
            remote(message, later.at[q], chip_send.at[q], chip_recv.at[q], ctx=sibling).wait_recv()
            for j in range(half):
                half_in[j] = later[q, j, :STATE] + later[q, j, STATE : STATE + 1] * half_in[j]

    hand_over = remote(half_in, sib_half, swap_sem.at[2], swap_sem.at[3], ctx=sibling)
    hand_over.start()
    hand_over.wait_recv()
    for j in range(half):
        for h, total in ((core * half + j, half_in[j]), ((1 - core) * half + j, sib_half[j])):
            nearer = sib_part[h, :STATE] + sib_part[h, STATE : STATE + 1] * total
            in_ref[h] = jnp.where(core == 1, total, nearer)

    def own_sent(c):
        pl.when(has_left)(lambda: own_copy(c, 0).wait_send())
        pl.when(has_right)(lambda: own_copy(c, 1).wait_send())

    each(count, own_sent)
    if paired:

        @pl.when(inner)
        def _():
            for q in range(chips):
                pl.when(q != chip)(lambda q=q: piece_peer(q).wait_send())
                piece_pair(q).wait_send()

            def passed(c):
                relay(end, c, mate).wait_send()
                sum_copy(c).wait_send()

            each(count, passed)

        pl.when(outer)(lambda: piece_down().wait_send())
    else:
        for d in range(1, tp):

            def passed(c):
                pl.when(jnp.logical_and(z >= d, has_right))(lambda: relay(z - d, c, z + 1).wait_send())
                pl.when(jnp.logical_and(z + d < tp, has_left))(lambda: relay(z + d, c, z - 1).wait_send())

            each(count, passed)
    swap.wait_send()
    for q in range(chips):
        pl.when(q < chip)(lambda q=q: chip_copy(q).wait_send())
    hand_over.wait_send()


def projected(upstream, out_weight, head_bc, log_decay):
    tp, ctx = lax.axis_size("tp"), lax.axis_size("ctx")
    tokens, depth = upstream.shape
    heads = log_decay.shape[0]
    width, chips, count = heads * HEAD_DIM, ctx // 2, tokens // CHUNK
    paired = tp == 4
    dma = pltpu.SemaphoreType.DMA
    anywhere = pl.BlockSpec(memory_space=pl.ANY)
    vmem = pl.BlockSpec(memory_space=pltpu.VMEM)
    packed = STATE + 8
    sums = (tokens, width) if paired else (16, 128)
    return pl.pallas_call(
        functools.partial(project_kernel, tp, ctx),
        out_shape=(
            jax.ShapeDtypeStruct((tokens, width), BF16),
            jax.ShapeDtypeStruct((heads, STATE, HEAD_DIM), F32),
        ),
        in_specs=[anywhere, anywhere, anywhere, vmem],
        out_specs=(vmem, vmem),
        scratch_shapes=[
            pltpu.VMEM((tp, tokens, depth), BF16),
            pltpu.VMEM(out_weight.shape, BF16),
            pltpu.VMEM(head_bc.shape, BF16),
            pltpu.VMEM((width, 2 * depth) if paired else (16, 128), BF16),
            pltpu.VMEM((tokens, width), F32),
            pltpu.VMEM(sums, BF16),
            pltpu.VMEM(sums, BF16),
            pltpu.VMEM((heads * STATE, tokens), BF16),
            pltpu.VMEM((heads, packed, HEAD_DIM), F32),
            pltpu.VMEM((heads, packed, HEAD_DIM), F32),
            pltpu.VMEM((heads // 2, packed, HEAD_DIM), F32),
            pltpu.VMEM((chips, heads // 2, packed, HEAD_DIM), F32),
            pltpu.VMEM((heads // 2, STATE, HEAD_DIM), F32),
            pltpu.VMEM((heads // 2, STATE, HEAD_DIM), F32),
            dma((3,)),
            dma((2, count)),
            dma((tp, count)),
            dma((tp, count)),
            dma((count,)),
            dma((count,)),
            dma,
            dma((chips,)),
            dma((chips,)),
            dma((ctx,)),
            dma((4,)),
            dma((chips,)),
            dma((chips,)),
        ],
        compiler_params=pltpu.CompilerParams(
            collective_id=0, has_side_effects=True, vmem_limit_bytes=56 * 1024 * 1024
        ),
        name="project_and_exchange",
    )(upstream, out_weight, head_bc, log_decay)


def block_kernel(
    heads, x_ref, bc_ref, dy_ref, log_ref, s_ref, skip_ref, in_ref, gx_ref, gbc_ref, glog_ref, h_ref
):
    @pl.when(pl.program_id(0) == 0)
    def _():
        h_ref[...] = in_ref[...]

    rows, cols = cumulative(log_ref[...])
    decay = jnp.exp(cols)
    tail = jnp.exp(cols[BLOCK - 1 : BLOCK, :] - cols)
    k_ids = lax.broadcasted_iota(jnp.int32, (BLOCK, BLOCK), 0)
    q_ids = lax.broadcasted_iota(jnp.int32, (BLOCK, BLOCK), 1)
    causal = q_ids >= k_ids
    sign = jnp.where(lax.broadcasted_iota(jnp.int32, (1, 128), 1) < STATE, -1.0, 1.0)
    lane = lax.broadcasted_iota(jnp.int32, (BLOCK, heads), 1)
    token = lax.broadcasted_iota(jnp.int32, (BLOCK, 1), 0)
    dcum = jnp.zeros((BLOCK, heads), F32)
    for h in range(heads):
        here = slice(h * 128, (h + 1) * 128)
        bc = bc_ref[:, here]
        b_rows, c_rows = bc[:, :STATE], bc[:, STATE:]
        x, dy = x_ref[:, here], dy_ref[:, here]
        carried, start = h_ref[h], s_ref[0, h]
        held, start_low = carried.astype(BF16), start.astype(BF16)
        gap = rows[h : h + 1, :] - cols[:, h : h + 1]
        gate = jnp.exp(jnp.where(causal, gap, -1e30))
        scores = lax.dot_general(b_rows, c_rows, LANES, preferred_element_type=F32) * gate
        inner = lax.dot_general(x, dy, LANES, preferred_element_type=F32) * gate
        scores, inner = scores.astype(BF16), inner.astype(BF16)
        tail_h, decay_h = tail[:, h : h + 1], decay[:, h : h + 1]
        gx = jnp.dot(scores, dy, preferred_element_type=F32)
        gx += tail_h * jnp.dot(b_rows, held, preferred_element_type=F32)
        gx += skip_ref[h] * dy.astype(F32)
        gx_ref[:, here] = gx.astype(BF16)
        gb_tail = tail_h * lax.dot_general(x, held, LANES, preferred_element_type=F32)
        gb = jnp.dot(inner, c_rows, preferred_element_type=F32) + gb_tail
        gc = lax.dot_general(inner, b_rows, ROWS, preferred_element_type=F32)
        gc += decay_h * lax.dot_general(dy, start_low, LANES, preferred_element_type=F32)
        gbc = jnp.concatenate([gb, gc], axis=1)
        gbc_ref[:, here] = gbc
        dcum_h = jnp.sum(bc.astype(F32) * gbc * sign, axis=1, keepdims=True)
        whole = decay[BLOCK - 1 : BLOCK, h : h + 1]
        at_end = whole * jnp.sum(start * carried) + jnp.sum(b_rows.astype(F32) * gb_tail)
        dcum_h = dcum_h + jnp.where(token == BLOCK - 1, at_end, 0.0)
        dcum = jnp.where(lane == h, dcum_h, dcum)
        h_ref[h] = whole * carried + later_terms(c_rows, dy, decay_h)
    from_here = jnp.where(k_ids >= q_ids, 1.0, 0.0)
    glog_ref[...] = jnp.dot(
        dcum.T, from_here, precision=lax.Precision.HIGHEST, preferred_element_type=F32
    )


def per_device(upstream, out_weight, inner_act, head_bc, log_decay, states, skip):
    tokens, heads = inner_act.shape[0], log_decay.shape[0]
    width = heads * HEAD_DIM
    blocks = tokens // BLOCK
    out_grad, incoming = projected(upstream, out_weight, head_bc, log_decay)
    wide = pl.BlockSpec((BLOCK, width), lambda i: (blocks - 1 - i, 0))
    logs = pl.BlockSpec((heads, BLOCK), lambda i: (0, blocks - 1 - i))
    carry = pl.BlockSpec((heads, STATE, HEAD_DIM), lambda i: (0, 0, 0))
    params = pltpu.CompilerParams(
        dimension_semantics=("arbitrary",), vmem_limit_bytes=48 * 1024 * 1024
    )
    return pl.pallas_call(
        functools.partial(block_kernel, heads),
        out_shape=(
            jax.ShapeDtypeStruct((tokens, width), BF16),
            jax.ShapeDtypeStruct((tokens, width), F32),
            jax.ShapeDtypeStruct((heads, tokens), F32),
        ),
        grid=(blocks,),
        in_specs=[
            wide,
            wide,
            wide,
            logs,
            pl.BlockSpec((1, heads, STATE, HEAD_DIM), lambda i: (blocks - 1 - i, 0, 0, 0)),
            pl.BlockSpec(memory_space=pltpu.SMEM),
            carry,
        ],
        out_specs=(wide, wide, logs),
        scratch_shapes=[pltpu.VMEM((heads, STATE, HEAD_DIM), F32)],
        compiler_params=params,
        name="block_gradients",
    )(inner_act, head_bc, out_grad, log_decay, states, skip, incoming)


def solution(mesh):
    return jax.shard_map(
        per_device,
        mesh=mesh,
        in_specs=(
            P("ctx", "tp"),
            P("tp", None),
            P("ctx", "tp"),
            P("ctx", "tp"),
            P("tp", "ctx"),
            P("ctx", "tp", None, None),
            P("tp"),
        ),
        out_specs=(P("ctx", "tp"), P("ctx", "tp"), P("tp", "ctx")),
        check_vma=False,
    )
```

```python
import functools

import jax
import jax.numpy as jnp
from jax import lax
from jax.experimental import pallas as pl
from jax.experimental.pallas import tpu as pltpu
from jax.sharding import PartitionSpec as P

HEAD_DIM = 128
STATE = 64
BLOCK = 256
CHUNK = 64
PER = BLOCK // CHUNK
F32 = jnp.float32
BF16 = jnp.bfloat16
ROWS = (((0,), (0,)), ((), ()))
LANES = (((1,), (1,)), ((), ()))


def cumulative(log_rows):
    earlier = lax.broadcasted_iota(jnp.int32, (BLOCK, BLOCK), 0)
    later = lax.broadcasted_iota(jnp.int32, (BLOCK, BLOCK), 1)
    upto = jnp.where(earlier <= later, 1.0, 0.0)
    rows = jnp.dot(log_rows, upto, precision=lax.Precision.HIGHEST, preferred_element_type=F32)
    return rows, rows.T


def part_combined(first, second):
    first_decay = first[STATE : STATE + 1]
    terms = first[:STATE] + first_decay * second[:STATE]
    return jnp.concatenate([terms, first[STATE:] * second[STATE:]], axis=0)


def project_kernel(
    tp,
    ctx,
    up_hbm,
    w_hbm,
    bc_hbm,
    log_ref,
    x_hbm,
    s_hbm,
    skip_ref,
    gx_hbm,
    gbc_hbm,
    term_hbm,
    in_ref,
    got,
    w_ref,
    bc_ref,
    far_w,
    acc,
    sum_out,
    sum_in,
    weighted,
    x_ref,
    s_ref,
    dy_ref,
    gx_ref,
    gbc_ref,
    term_ref,
    cum_rows,
    cum_cols,
    part,
    sib_part,
    message,
    later,
    half_in,
    sib_half,
    local_sem,
    own_sem,
    relay_sem,
    got_sem,
    sum_send,
    sum_recv,
    piece_sem,
    peer_sem,
    pair_sem,
    far_sem,
    swap_sem,
    chip_send,
    chip_recv,
    out_sem,
):
    z, me = lax.axis_index("tp"), lax.axis_index("ctx")
    core, chip = lax.rem(me, 2), lax.div(me, 2)
    sibling = me + 1 - 2 * core
    chips = ctx // 2
    heads = log_ref.shape[0]
    half = heads // 2
    tokens, depth = up_hbm.shape
    width = w_hbm.shape[0]
    piece = width // ctx
    count = tokens // CHUNK
    blocks = tokens // BLOCK
    paired = tp == 4
    has_left, has_right = z > 0, z < tp - 1
    inner = jnp.logical_and(has_left, has_right)
    outer = jnp.logical_not(inner)

    def rows_of(c):
        return pl.ds(pl.multiple_of(c * CHUNK, CHUNK), CHUNK)

    def remote(src, dst, send, recv, **place):
        return pltpu.make_async_remote_copy(
            src_ref=src,
            dst_ref=dst,
            send_sem=send,
            recv_sem=recv,
            device_id=place,
            device_id_type=pl.DeviceIdType.MESH,
        )

    def own_copy(c, side):
        target = z - 1 if side == 0 else z + 1
        return remote(
            up_hbm.at[rows_of(c)], got.at[z, rows_of(c)], own_sem.at[side, c], got_sem.at[z, c], tp=target
        )

    def relay(s, c, target):
        place = got.at[s, rows_of(c)]
        return remote(place, place, relay_sem.at[s, c], got_sem.at[s, c], tp=target)

    def each(n, body):
        lax.fori_loop(0, n, lambda c, unused: (body(c), unused)[1], 0)

    def term(s, c):
        columns = pl.ds(pl.multiple_of(s * depth, depth), depth)
        return lax.dot_general(got[s, rows_of(c)], w_ref[:, columns], LANES, preferred_element_type=F32)

    load_w = pltpu.make_async_copy(w_hbm, w_ref, local_sem.at[0])
    load_up = pltpu.make_async_copy(up_hbm, got.at[z], local_sem.at[1])
    load_bc = pltpu.make_async_copy(bc_hbm, bc_ref, local_sem.at[2])
    load_up.start()
    load_w.start()
    load_bc.start()
    load_x = pltpu.make_async_copy(x_hbm, x_ref, local_sem.at[3])
    load_s = pltpu.make_async_copy(s_hbm, s_ref, local_sem.at[4])
    load_x.start()
    load_s.start()

    barrier = pltpu.get_barrier_semaphore()

    def greet(**place):
        pl.semaphore_signal(barrier, inc=1, device_id=place, device_id_type=pl.DeviceIdType.MESH)

    pl.when(has_left)(lambda: greet(tp=z - 1))
    pl.when(has_right)(lambda: greet(tp=z + 1))
    greet(ctx=sibling)
    for q in range(chips):
        pl.when(q != chip)(functools.partial(greet, ctx=2 * q + core))
    pl.semaphore_wait(barrier, chips + has_left.astype(jnp.int32) + has_right.astype(jnp.int32))

    low = jnp.where(z <= 1, 2, 0)

    def piece_place(j):
        return far_w.at[pl.ds(pl.multiple_of(j * piece, piece), piece)]

    def piece_down():
        source = w_hbm.at[
            pl.ds(pl.multiple_of(me * piece, piece), piece),
            pl.ds(pl.multiple_of(low * depth, depth), 2 * depth),
        ]
        return remote(source, piece_place(me), piece_sem, far_sem.at[me], tp=jnp.where(z == 0, 1, tp - 2))

    def piece_peer(q):
        place = piece_place(me)
        return remote(place, place, peer_sem.at[q], far_sem.at[me], ctx=2 * q + core)

    def piece_pair(q):
        place = piece_place(2 * q + core)
        return remote(place, place, pair_sem.at[q], far_sem.at[2 * q + core], ctx=sibling)

    def piece_wait(j):
        remote(piece_place(j), piece_place(j), piece_sem, far_sem.at[j], ctx=sibling).wait_recv()

    if paired:
        pl.when(outer)(lambda: piece_down().start())

    def send_own(c):
        early = jnp.logical_or(c < count // 2, not paired)
        pl.when(jnp.logical_and(has_left, jnp.logical_or(early, z != 2)))(lambda: own_copy(c, 0).start())
        pl.when(jnp.logical_and(has_right, jnp.logical_or(early, z != 1)))(lambda: own_copy(c, 1).start())

    each(count, send_own)
    load_up.wait()
    load_w.wait()

    def own_term(c):
        acc[rows_of(c)] = term(z, c)

    each(count, own_term)

    if paired:

        @pl.when(inner)
        def _():
            piece_wait(me)
            for q in range(chips):
                pl.when(q != chip)(lambda q=q: piece_peer(q).start())
            piece_pair(chip).start()

    load_bc.wait()

    def rows_of_block(b):
        return pl.ds(pl.multiple_of(b * BLOCK, BLOCK), BLOCK)

    def weigh(b):
        here = rows_of_block(b)
        rows, cols = cumulative(log_ref[:, here])
        cum_rows[:, here] = rows
        cum_cols[here] = cols
        decay = jnp.exp(rows)
        for h in range(heads):
            c_rows = bc_ref[here, h * 128 : (h + 1) * 128].astype(F32).T[STATE:]
            weighted[h * STATE : (h + 1) * STATE, here] = (c_rows * decay[h : h + 1]).astype(BF16)

    each(blocks, weigh)
    load_x.wait()
    load_s.wait()

    def block_terms(b):
        here = rows_of_block(b)
        for h in range(heads):
            term_ref[b, h] = jnp.dot(
                weighted[h * STATE : (h + 1) * STATE, here],
                dy_ref[here, h * 128 : (h + 1) * 128],
                preferred_element_type=F32,
            )

    k_ids = lax.broadcasted_iota(jnp.int32, (BLOCK, BLOCK), 0)
    q_ids = lax.broadcasted_iota(jnp.int32, (BLOCK, BLOCK), 1)

    def local_gradients(b, group):
        here = rows_of_block(b)
        for h in range(group * heads // PER, (group + 1) * heads // PER):
            at = slice(h * 128, (h + 1) * 128)
            bc, x, dy = bc_ref[here, at], x_ref[here, at], dy_ref[here, at]
            b_rows, c_rows = bc[:, :STATE], bc[:, STATE:]
            column = cum_cols[here, h : h + 1]
            gap = cum_rows[h : h + 1, here] - column
            gate = jnp.exp(jnp.where(q_ids >= k_ids, gap, -1e30))
            scores = lax.dot_general(b_rows, c_rows, LANES, preferred_element_type=F32) * gate
            inside = lax.dot_general(x, dy, LANES, preferred_element_type=F32) * gate
            scores, inside = scores.astype(BF16), inside.astype(BF16)
            gx = jnp.dot(scores, dy, preferred_element_type=F32)
            gx_ref[here, at] = gx + skip_ref[h] * dy.astype(F32)
            gb = jnp.dot(inside, c_rows, preferred_element_type=F32)
            gc = lax.dot_general(inside, b_rows, ROWS, preferred_element_type=F32)
            start = s_ref[b, h].astype(BF16)
            gc += jnp.exp(column) * lax.dot_general(dy, start, LANES, preferred_element_type=F32)
            gbc_ref[here, at] = jnp.concatenate([gb, gc], axis=1)

    def out_copies(b):
        here = rows_of_block(b)
        return (
            pltpu.make_async_copy(gx_ref.at[here], gx_hbm.at[here], out_sem.at[0, b]),
            pltpu.make_async_copy(gbc_ref.at[here], gbc_hbm.at[here], out_sem.at[1, b]),
        )

    def send_out(b):
        for copy in out_copies(b):
            copy.start()

    def drain(arrive):
        def take(b):
            for i in range(PER):
                dy_ref[rows_of(b * PER + i)] = arrive(b, b * PER + i).astype(BF16)
                pl.when(b > 0)(functools.partial(local_gradients, b - 1, i))
            pl.when(b > 0)(lambda: send_out(b - 1))
            block_terms(b)

        each(blocks, take)

    if paired:
        end = jnp.where(z == 1, 0, 3)
        mate, far = 3 - z, 3 - end
        next_in = jnp.where(z == 0, 1, tp - 2)

        def sum_copy(c):
            return remote(
                sum_out.at[rows_of(c)], sum_in.at[rows_of(c)], sum_send.at[c], sum_recv.at[c], tp=end
            )

        def first_hop(c):
            relay(end, c, mate).wait_recv()
            relay(end, c, mate).start()

            @pl.when(c < count - count // 2)
            def _():
                pl.when(z == 2)(lambda: own_copy(c + count // 2, 0).start())
                pl.when(z == 1)(lambda: own_copy(c + count // 2, 1).start())

            acc[rows_of(c)] += term(end, c)

        def second_hop(b, c):
            early = c + count // 2
            pl.when(early < count)(lambda: first_hop(early))
            relay(mate, c, mate).wait_recv()
            relay(far, c, mate).wait_recv()
            outward = lax.dot_general(
                got[low, rows_of(c)], far_w[:, :depth], LANES, preferred_element_type=F32
            )
            outward += lax.dot_general(
                got[low + 1, rows_of(c)], far_w[:, depth:], LANES, preferred_element_type=F32
            )
            sum_out[rows_of(c)] = outward.astype(BF16)
            sum_copy(c).start()
            return acc[rows_of(c)] + term(mate, c) + term(far, c)

        @pl.when(inner)
        def _():
            each(count // 2, first_hop)
            for q in range(chips):

                @pl.when(q != chip)
                def _():
                    piece_wait(2 * q + core)
                    piece_pair(q).start()

            for q in range(chips):
                piece_wait(2 * q + 1 - core)
            drain(second_hop)

        def one_hop(c):
            relay(next_in, c, next_in).wait_recv()
            acc[rows_of(c)] += term(next_in, c)

        def last_sum(b, c):
            sum_copy(c).wait_recv()
            return acc[rows_of(c)] + sum_in[rows_of(c)].astype(F32)

        @pl.when(outer)
        def _():
            each(count, one_hop)
            drain(last_sum)

    else:
        for d in range(1, tp):

            def hop(c):
                @pl.when(z >= d)
                def _():
                    relay(z - d, c, z + 1).wait_recv()
                    pl.when(has_right)(lambda: relay(z - d, c, z + 1).start())
                    acc[rows_of(c)] += term(z - d, c)

                @pl.when(z + d < tp)
                def _():
                    relay(z + d, c, z - 1).wait_recv()
                    pl.when(has_left)(lambda: relay(z + d, c, z - 1).start())
                    acc[rows_of(c)] += term(z + d, c)

            each(count, hop)
        drain(lambda b, c: acc[rows_of(c)])

    for h in range(heads):
        total, decay = term_ref[blocks - 1, h], 0.0
        for b in reversed(range(blocks)):
            log = cum_rows[h : h + 1, (b + 1) * BLOCK - 1 : (b + 1) * BLOCK]
            decay = decay + log
            if b < blocks - 1:
                total = term_ref[b, h] + jnp.exp(log) * total
        part[h, :STATE] = total
        part[h, STATE:] = jnp.broadcast_to(jnp.exp(decay), (8, HEAD_DIM))
    term_copy = pltpu.make_async_copy(term_ref, term_hbm, local_sem.at[5])
    term_copy.start()

    swap = remote(part, sib_part, swap_sem.at[0], swap_sem.at[1], ctx=sibling)
    swap.start()
    local_gradients(blocks - 1, 0)
    swap.wait_recv()
    for j in range(half):
        mine, other = part[core * half + j], sib_part[core * half + j]
        first, second = jnp.where(core == 0, mine, other), jnp.where(core == 0, other, mine)
        message[j] = part_combined(first, second)

    def chip_copy(q):
        return remote(message, later.at[chip], chip_send.at[q], chip_recv.at[chip], ctx=2 * q + core)

    for q in reversed(range(chips)):
        pl.when(q < chip)(lambda q=q: chip_copy(q).start())
    half_in[...] = jnp.zeros_like(half_in)
    local_gradients(blocks - 1, 1)
    local_gradients(blocks - 1, 2)
    for q in reversed(range(chips)):

        @pl.when(q > chip)
        def _():
            remote(message, later.at[q], chip_send.at[q], chip_recv.at[q], ctx=sibling).wait_recv()
            for j in range(half):
                half_in[j] = later[q, j, :STATE] + later[q, j, STATE : STATE + 1] * half_in[j]

    hand_over = remote(half_in, sib_half, swap_sem.at[2], swap_sem.at[3], ctx=sibling)
    hand_over.start()
    local_gradients(blocks - 1, 3)
    send_out(blocks - 1)
    hand_over.wait_recv()
    for j in range(half):
        for h, total in ((core * half + j, half_in[j]), ((1 - core) * half + j, sib_half[j])):
            nearer = sib_part[h, :STATE] + sib_part[h, STATE : STATE + 1] * total
            in_ref[h] = jnp.where(core == 1, total, nearer)

    def own_sent(c):
        pl.when(has_left)(lambda: own_copy(c, 0).wait_send())
        pl.when(has_right)(lambda: own_copy(c, 1).wait_send())

    each(count, own_sent)
    if paired:

        @pl.when(inner)
        def _():
            for q in range(chips):
                pl.when(q != chip)(lambda q=q: piece_peer(q).wait_send())
                piece_pair(q).wait_send()

            def passed(c):
                relay(end, c, mate).wait_send()
                sum_copy(c).wait_send()

            each(count, passed)

        pl.when(outer)(lambda: piece_down().wait_send())
    else:
        for d in range(1, tp):

            def passed(c):
                pl.when(jnp.logical_and(z >= d, has_right))(lambda: relay(z - d, c, z + 1).wait_send())
                pl.when(jnp.logical_and(z + d < tp, has_left))(lambda: relay(z + d, c, z - 1).wait_send())

            each(count, passed)
    swap.wait_send()
    for q in range(chips):
        pl.when(q < chip)(lambda q=q: chip_copy(q).wait_send())
    hand_over.wait_send()
    term_copy.wait()
    for b in range(blocks):
        for copy in out_copies(b):
            copy.wait()


def projected(upstream, out_weight, inner_act, head_bc, log_decay, states, skip):
    tp, ctx = lax.axis_size("tp"), lax.axis_size("ctx")
    tokens, depth = upstream.shape
    heads = log_decay.shape[0]
    width, chips, count = heads * HEAD_DIM, ctx // 2, tokens // CHUNK
    paired = tp == 4
    dma = pltpu.SemaphoreType.DMA
    anywhere = pl.BlockSpec(memory_space=pl.ANY)
    vmem = pl.BlockSpec(memory_space=pltpu.VMEM)
    packed = STATE + 8
    sums = (tokens, width) if paired else (16, 128)
    return pl.pallas_call(
        functools.partial(project_kernel, tp, ctx),
        out_shape=(
            jax.ShapeDtypeStruct((tokens, width), F32),
            jax.ShapeDtypeStruct((tokens, width), F32),
            jax.ShapeDtypeStruct(states.shape, F32),
            jax.ShapeDtypeStruct((heads, STATE, HEAD_DIM), F32),
        ),
        in_specs=[
            anywhere,
            anywhere,
            anywhere,
            vmem,
            anywhere,
            anywhere,
            pl.BlockSpec(memory_space=pltpu.SMEM),
        ],
        out_specs=(anywhere, anywhere, anywhere, vmem),
        scratch_shapes=[
            pltpu.VMEM((tp, tokens, depth), BF16),
            pltpu.VMEM(out_weight.shape, BF16),
            pltpu.VMEM(head_bc.shape, BF16),
            pltpu.VMEM((width, 2 * depth) if paired else (16, 128), BF16),
            pltpu.VMEM((tokens, width), F32),
            pltpu.VMEM(sums, BF16),
            pltpu.VMEM(sums, BF16),
            pltpu.VMEM((heads * STATE, tokens), BF16),
            pltpu.VMEM((tokens, width), BF16),
            pltpu.VMEM(states.shape, F32),
            pltpu.VMEM((tokens, width), BF16),
            pltpu.VMEM((tokens, width), F32),
            pltpu.VMEM((tokens, width), F32),
            pltpu.VMEM(states.shape, F32),
            pltpu.VMEM((heads, tokens), F32),
            pltpu.VMEM((tokens, heads), F32),
            pltpu.VMEM((heads, packed, HEAD_DIM), F32),
            pltpu.VMEM((heads, packed, HEAD_DIM), F32),
            pltpu.VMEM((heads // 2, packed, HEAD_DIM), F32),
            pltpu.VMEM((chips, heads // 2, packed, HEAD_DIM), F32),
            pltpu.VMEM((heads // 2, STATE, HEAD_DIM), F32),
            pltpu.VMEM((heads // 2, STATE, HEAD_DIM), F32),
            dma((6,)),
            dma((2, count)),
            dma((tp, count)),
            dma((tp, count)),
            dma((count,)),
            dma((count,)),
            dma,
            dma((chips,)),
            dma((chips,)),
            dma((ctx,)),
            dma((4,)),
            dma((chips,)),
            dma((chips,)),
            dma((2, tokens // BLOCK)),
        ],
        compiler_params=pltpu.CompilerParams(
            collective_id=0, has_side_effects=True, vmem_limit_bytes=56 * 1024 * 1024
        ),
        name="project_and_exchange",
    )(upstream, out_weight, head_bc, log_decay, inner_act, states, skip)


def closing_kernel(
    heads, x_ref, bc_ref, gx0_ref, gbc0_ref, log_ref, s_ref, term_ref, in_ref, gx_ref, gbc_ref, glog_ref, h_ref
):
    @pl.when(pl.program_id(0) == 0)
    def _():
        h_ref[...] = in_ref[...]

    rows, cols = cumulative(log_ref[...])
    last = cols[BLOCK - 1 : BLOCK, :]
    whole, tail = jnp.exp(last), jnp.exp(last - cols)
    sign = jnp.where(lax.broadcasted_iota(jnp.int32, (1, 128), 1) < STATE, -1.0, 1.0)
    lane = lax.broadcasted_iota(jnp.int32, (BLOCK, heads), 1)
    token = lax.broadcasted_iota(jnp.int32, (BLOCK, 1), 0)
    dcum = jnp.zeros((BLOCK, heads), F32)
    for h in range(heads):
        here = slice(h * 128, (h + 1) * 128)
        bc = bc_ref[:, here]
        carried = h_ref[h]
        held = carried.astype(BF16)
        tail_h, whole_h = tail[:, h : h + 1], whole[:, h : h + 1]
        added = jnp.dot(bc[:, :STATE], held, preferred_element_type=F32)
        gx_ref[:, here] = (gx0_ref[:, here] + tail_h * added).astype(BF16)
        gb_tail = tail_h * lax.dot_general(x_ref[:, here], held, LANES, preferred_element_type=F32)
        wide_tail = jnp.concatenate([gb_tail, jnp.zeros_like(gb_tail)], axis=1)
        gbc = gbc0_ref[:, here] + wide_tail
        gbc_ref[:, here] = gbc
        bc_wide = bc.astype(F32)
        dcum_h = jnp.sum(bc_wide * gbc * sign, axis=1, keepdims=True)
        at_end = whole_h * jnp.sum(s_ref[0, h] * carried) + jnp.sum(bc_wide * wide_tail)
        dcum_h = dcum_h + jnp.where(token == BLOCK - 1, at_end, 0.0)
        dcum = jnp.where(lane == h, dcum_h, dcum)
        h_ref[h] = whole_h * carried + term_ref[0, h]
    s_ids = lax.broadcasted_iota(jnp.int32, (BLOCK, BLOCK), 0)
    t_ids = lax.broadcasted_iota(jnp.int32, (BLOCK, BLOCK), 1)
    from_here = jnp.where(s_ids >= t_ids, 1.0, 0.0)
    glog_ref[...] = jnp.dot(
        dcum.T, from_here, precision=lax.Precision.HIGHEST, preferred_element_type=F32
    )


def per_device(upstream, out_weight, inner_act, head_bc, log_decay, states, skip):
    tokens, heads = inner_act.shape[0], log_decay.shape[0]
    width = heads * HEAD_DIM
    blocks = tokens // BLOCK
    gx, gbc, terms, incoming = projected(
        upstream, out_weight, inner_act, head_bc, log_decay, states, skip
    )
    wide = pl.BlockSpec((BLOCK, width), lambda i: (blocks - 1 - i, 0))
    logs = pl.BlockSpec((heads, BLOCK), lambda i: (0, blocks - 1 - i))
    block = pl.BlockSpec((1, heads, STATE, HEAD_DIM), lambda i: (blocks - 1 - i, 0, 0, 0))
    carry = pl.BlockSpec((heads, STATE, HEAD_DIM), lambda i: (0, 0, 0))
    params = pltpu.CompilerParams(
        dimension_semantics=("arbitrary",), vmem_limit_bytes=48 * 1024 * 1024
    )
    return pl.pallas_call(
        functools.partial(closing_kernel, heads),
        out_shape=(
            jax.ShapeDtypeStruct((tokens, width), BF16),
            jax.ShapeDtypeStruct((tokens, width), F32),
            jax.ShapeDtypeStruct((heads, tokens), F32),
        ),
        grid=(blocks,),
        in_specs=[
            wide,
            wide,
            wide,
            wide,
            logs,
            block,
            block,
            carry,
        ],
        out_specs=(wide, wide, logs),
        scratch_shapes=[pltpu.VMEM((heads, STATE, HEAD_DIM), F32)],
        compiler_params=params,
        name="carried_terms",
    )(inner_act, head_bc, gx, gbc, log_decay, states, terms, incoming)


def solution(mesh):
    return jax.shard_map(
        per_device,
        mesh=mesh,
        in_specs=(
            P("ctx", "tp"),
            P("tp", None),
            P("ctx", "tp"),
            P("ctx", "tp"),
            P("tp", "ctx"),
            P("ctx", "tp", None, None),
            P("tp"),
        ),
        out_specs=(P("ctx", "tp"), P("ctx", "tp"), P("tp", "ctx")),
        check_vma=False,
    )
```

```python
import functools

import jax
import jax.numpy as jnp
from jax import lax
from jax.experimental import pallas as pl
from jax.experimental.pallas import tpu as pltpu
from jax.sharding import PartitionSpec as P

HEAD_DIM = 128
STATE = 64
BLOCK = 256
CHUNK = 64
PER = BLOCK // CHUNK
F32 = jnp.float32
BF16 = jnp.bfloat16
ROWS = (((0,), (0,)), ((), ()))
LANES = (((1,), (1,)), ((), ()))


def cumulative(log_rows):
    earlier = lax.broadcasted_iota(jnp.int32, (BLOCK, BLOCK), 0)
    later = lax.broadcasted_iota(jnp.int32, (BLOCK, BLOCK), 1)
    upto = jnp.where(earlier <= later, 1.0, 0.0)
    rows = jnp.dot(log_rows, upto, precision=lax.Precision.HIGHEST, preferred_element_type=F32)
    return rows, rows.T


def part_combined(first, second):
    first_decay = first[STATE : STATE + 1]
    terms = first[:STATE] + first_decay * second[:STATE]
    return jnp.concatenate([terms, first[STATE:] * second[STATE:]], axis=0)


def project_kernel(
    tp,
    ctx,
    up_hbm,
    w_hbm,
    bc_hbm,
    log_ref,
    x_hbm,
    s_hbm,
    skip_ref,
    gx_hbm,
    gbc_hbm,
    term_hbm,
    in_ref,
    got,
    w_ref,
    bc_ref,
    far_w,
    acc,
    mate_sum,
    sum_out,
    sum_in,
    weighted,
    x_ref,
    s_ref,
    dy_ref,
    gx_ref,
    gbc_ref,
    term_ref,
    cum_rows,
    cum_cols,
    part,
    sib_part,
    message,
    later,
    half_in,
    sib_half,
    local_sem,
    own_sem,
    relay_sem,
    got_sem,
    sum_send,
    sum_recv,
    piece_sem,
    peer_sem,
    pair_sem,
    far_sem,
    swap_sem,
    chip_send,
    chip_recv,
    out_sem,
):
    z, me = lax.axis_index("tp"), lax.axis_index("ctx")
    core, chip = lax.rem(me, 2), lax.div(me, 2)
    sibling = me + 1 - 2 * core
    chips = ctx // 2
    heads = log_ref.shape[0]
    half = heads // 2
    tokens, depth = up_hbm.shape
    width = w_hbm.shape[0]
    piece = width // ctx
    count = tokens // CHUNK
    blocks = tokens // BLOCK
    paired = tp == 4
    has_left, has_right = z > 0, z < tp - 1
    inner = jnp.logical_and(has_left, has_right)
    outer = jnp.logical_not(inner)
    low = jnp.where(z <= 1, 2, 0)

    def rows_of(c):
        return pl.ds(pl.multiple_of(c * CHUNK, CHUNK), CHUNK)

    def remote(src, dst, send, recv, **place):
        return pltpu.make_async_remote_copy(
            src_ref=src,
            dst_ref=dst,
            send_sem=send,
            recv_sem=recv,
            device_id=place,
            device_id_type=pl.DeviceIdType.MESH,
        )

    def own_copy(c, side):
        target = z - 1 if side == 0 else z + 1
        return remote(
            up_hbm.at[rows_of(c)], got.at[z, rows_of(c)], own_sem.at[side, c], got_sem.at[z, c], tp=target
        )

    def relay(s, c, target):
        place = got.at[s, rows_of(c)]
        return remote(place, place, relay_sem.at[s, c], got_sem.at[s, c], tp=target)

    def each(n, body):
        lax.fori_loop(0, n, lambda c, unused: (body(c), unused)[1], 0)

    def rows_of_block(b):
        return pl.ds(pl.multiple_of(b * BLOCK, BLOCK), BLOCK)

    def term(s, rows):
        columns = pl.ds(pl.multiple_of(s * depth, depth), depth)
        return lax.dot_general(got[s, rows], w_ref[:, columns], LANES, preferred_element_type=F32)

    def outward(s, rows):
        columns = pl.ds(pl.multiple_of((s - low) * depth, depth), depth)
        return lax.dot_general(got[s, rows], far_w[:, columns], LANES, preferred_element_type=F32)

    def add_term(s, b):
        acc[rows_of_block(b)] += term(s, rows_of_block(b))

    load_w = pltpu.make_async_copy(w_hbm, w_ref, local_sem.at[0])
    load_up = pltpu.make_async_copy(up_hbm, got.at[z], local_sem.at[1])
    load_bc = pltpu.make_async_copy(bc_hbm, bc_ref, local_sem.at[2])
    load_up.start()
    load_w.start()
    load_bc.start()
    load_x = pltpu.make_async_copy(x_hbm, x_ref, local_sem.at[3])
    load_s = pltpu.make_async_copy(s_hbm, s_ref, local_sem.at[4])
    load_x.start()
    load_s.start()

    barrier = pltpu.get_barrier_semaphore()

    def greet(**place):
        pl.semaphore_signal(barrier, inc=1, device_id=place, device_id_type=pl.DeviceIdType.MESH)

    pl.when(has_left)(lambda: greet(tp=z - 1))
    pl.when(has_right)(lambda: greet(tp=z + 1))
    greet(ctx=sibling)
    for q in range(chips):
        pl.when(q != chip)(functools.partial(greet, ctx=2 * q + core))
    pl.semaphore_wait(barrier, chips + has_left.astype(jnp.int32) + has_right.astype(jnp.int32))


    def piece_place(j):
        return far_w.at[pl.ds(pl.multiple_of(j * piece, piece), piece)]

    def piece_down():
        source = w_hbm.at[
            pl.ds(pl.multiple_of(me * piece, piece), piece),
            pl.ds(pl.multiple_of(low * depth, depth), 2 * depth),
        ]
        return remote(source, piece_place(me), piece_sem, far_sem.at[me], tp=jnp.where(z == 0, 1, tp - 2))

    def piece_peer(q):
        place = piece_place(me)
        return remote(place, place, peer_sem.at[q], far_sem.at[me], ctx=2 * q + core)

    def piece_pair(q):
        place = piece_place(2 * q + core)
        return remote(place, place, pair_sem.at[q], far_sem.at[2 * q + core], ctx=sibling)

    def piece_wait(j):
        remote(piece_place(j), piece_place(j), piece_sem, far_sem.at[j], ctx=sibling).wait_recv()

    if paired:
        pl.when(outer)(lambda: piece_down().start())

    def send_own(c):
        early = jnp.logical_or(c < count // 2, not paired)
        pl.when(jnp.logical_and(has_left, jnp.logical_or(early, z != 2)))(lambda: own_copy(c, 0).start())
        pl.when(jnp.logical_and(has_right, jnp.logical_or(early, z != 1)))(lambda: own_copy(c, 1).start())

    each(count, send_own)
    load_up.wait()
    load_w.wait()

    def own_term(b):
        acc[rows_of_block(b)] = term(z, rows_of_block(b))

    each(blocks, own_term)

    if paired:

        @pl.when(inner)
        def _():
            piece_wait(me)
            for q in range(chips):
                pl.when(q != chip)(lambda q=q: piece_peer(q).start())
            piece_pair(chip).start()

    load_bc.wait()

    def weigh(b):
        here = rows_of_block(b)
        rows, cols = cumulative(log_ref[:, here])
        cum_rows[:, here] = rows
        cum_cols[here] = cols
        decay = jnp.exp(rows)
        for h in range(heads):
            c_rows = bc_ref[here, h * 128 : (h + 1) * 128].astype(F32).T[STATE:]
            weighted[h * STATE : (h + 1) * STATE, here] = (c_rows * decay[h : h + 1]).astype(BF16)

    each(blocks, weigh)
    load_x.wait()
    load_s.wait()

    def block_terms(b):
        here = rows_of_block(b)
        for h in range(heads):
            term_ref[b, h] = jnp.dot(
                weighted[h * STATE : (h + 1) * STATE, here],
                dy_ref[here, h * 128 : (h + 1) * 128],
                preferred_element_type=F32,
            )

    k_ids = lax.broadcasted_iota(jnp.int32, (BLOCK, BLOCK), 0)
    q_ids = lax.broadcasted_iota(jnp.int32, (BLOCK, BLOCK), 1)

    def local_gradients(b, group):
        here = rows_of_block(b)
        for h in range(group * heads // PER, (group + 1) * heads // PER):
            at = slice(h * 128, (h + 1) * 128)
            bc, x, dy = bc_ref[here, at], x_ref[here, at], dy_ref[here, at]
            b_rows, c_rows = bc[:, :STATE], bc[:, STATE:]
            column = cum_cols[here, h : h + 1]
            gap = cum_rows[h : h + 1, here] - column
            gate = jnp.exp(jnp.where(q_ids >= k_ids, gap, -1e30))
            scores = lax.dot_general(b_rows, c_rows, LANES, preferred_element_type=F32) * gate
            inside = lax.dot_general(x, dy, LANES, preferred_element_type=F32) * gate
            scores, inside = scores.astype(BF16), inside.astype(BF16)
            gx = jnp.dot(scores, dy, preferred_element_type=F32)
            gx_ref[here, at] = gx + skip_ref[h] * dy.astype(F32)
            gb = jnp.dot(inside, c_rows, preferred_element_type=F32)
            gc = lax.dot_general(inside, b_rows, ROWS, preferred_element_type=F32)
            start = s_ref[b, h].astype(BF16)
            gc += jnp.exp(column) * lax.dot_general(dy, start, LANES, preferred_element_type=F32)
            gbc_ref[here, at] = jnp.concatenate([gb, gc], axis=1)

    def out_copies(b):
        here = rows_of_block(b)
        return (
            pltpu.make_async_copy(gx_ref.at[here], gx_hbm.at[here], out_sem.at[0, b]),
            pltpu.make_async_copy(gbc_ref.at[here], gbc_hbm.at[here], out_sem.at[1, b]),
        )

    def send_out(b):
        for copy in out_copies(b):
            copy.start()

    def drain(arrive, before=None, after=None):
        def take(b):
            if before is not None:
                before(b)
            for i in range(PER):
                dy_ref[rows_of(b * PER + i)] = arrive(b, b * PER + i).astype(BF16)
                pl.when(b > 0)(functools.partial(local_gradients, b - 1, i))
            pl.when(b > 0)(lambda: send_out(b - 1))
            block_terms(b)
            if after is not None:
                after(b)

        each(blocks, take)

    if paired:
        end = jnp.where(z == 1, 0, 3)
        mate, far = 3 - z, 3 - end
        next_in = jnp.where(z == 0, 1, tp - 2)

        def sum_copy(c):
            return remote(
                sum_out.at[rows_of(c)], sum_in.at[rows_of(c)], sum_send.at[c], sum_recv.at[c], tp=end
            )

        def first_hop(c):
            relay(end, c, mate).wait_recv()
            relay(end, c, mate).start()

            @pl.when(c < count - count // 2)
            def _():
                pl.when(z == 2)(lambda: own_copy(c + count // 2, 0).start())
                pl.when(z == 1)(lambda: own_copy(c + count // 2, 1).start())

        first_blocks = (blocks + 1) // 2

        def first_block(b):
            for i in range(PER):
                first_hop(b * PER + i)
            add_term(end, b)

        def mate_block(b):
            for i in range(PER):
                relay(mate, b * PER + i, mate).wait_recv()
            add_term(mate, b)
            mate_sum[...] = outward(mate, rows_of_block(b))

        def second_hop(b, c):
            pl.when(b < blocks - first_blocks)(lambda: first_hop(c + first_blocks * PER))
            relay(far, c, mate).wait_recv()
            in_block = pl.ds(pl.multiple_of((c - b * PER) * CHUNK, CHUNK), CHUNK)
            sum_out[rows_of(c)] = (mate_sum[in_block] + outward(far, rows_of(c))).astype(BF16)
            sum_copy(c).start()
            return acc[rows_of(c)] + term(far, rows_of(c))

        def late_block(b):
            pl.when(b < blocks - first_blocks)(lambda: add_term(end, b + first_blocks))

        @pl.when(inner)
        def _():
            each(first_blocks, first_block)
            for q in range(chips):

                @pl.when(q != chip)
                def _():
                    piece_wait(2 * q + core)
                    piece_pair(q).start()

            for q in range(chips):
                piece_wait(2 * q + 1 - core)
            drain(second_hop, mate_block, late_block)

        def one_hop(b):
            for i in range(PER):
                relay(next_in, b * PER + i, next_in).wait_recv()
            add_term(next_in, b)

        def last_sum(b, c):
            sum_copy(c).wait_recv()
            return acc[rows_of(c)] + sum_in[rows_of(c)].astype(F32)

        @pl.when(outer)
        def _():
            each(blocks, one_hop)
            drain(last_sum)

    else:
        for d in range(1, tp):

            def hop(c):
                @pl.when(z >= d)
                def _():
                    relay(z - d, c, z + 1).wait_recv()
                    pl.when(has_right)(lambda: relay(z - d, c, z + 1).start())
                    acc[rows_of(c)] += term(z - d, rows_of(c))

                @pl.when(z + d < tp)
                def _():
                    relay(z + d, c, z - 1).wait_recv()
                    pl.when(has_left)(lambda: relay(z + d, c, z - 1).start())
                    acc[rows_of(c)] += term(z + d, rows_of(c))

            each(count, hop)
        drain(lambda b, c: acc[rows_of(c)])

    for h in range(heads):
        total, decay = term_ref[blocks - 1, h], 0.0
        for b in reversed(range(blocks)):
            log = cum_rows[h : h + 1, (b + 1) * BLOCK - 1 : (b + 1) * BLOCK]
            decay = decay + log
            if b < blocks - 1:
                total = term_ref[b, h] + jnp.exp(log) * total
        part[h, :STATE] = total
        part[h, STATE:] = jnp.broadcast_to(jnp.exp(decay), (8, HEAD_DIM))
    term_copy = pltpu.make_async_copy(term_ref, term_hbm, local_sem.at[5])
    term_copy.start()

    swap = remote(part, sib_part, swap_sem.at[0], swap_sem.at[1], ctx=sibling)
    swap.start()
    local_gradients(blocks - 1, 0)
    swap.wait_recv()
    for j in range(half):
        mine, other = part[core * half + j], sib_part[core * half + j]
        first, second = jnp.where(core == 0, mine, other), jnp.where(core == 0, other, mine)
        message[j] = part_combined(first, second)

    def chip_copy(q):
        return remote(message, later.at[chip], chip_send.at[q], chip_recv.at[chip], ctx=2 * q + core)

    for q in reversed(range(chips)):
        pl.when(q < chip)(lambda q=q: chip_copy(q).start())
    half_in[...] = jnp.zeros_like(half_in)
    local_gradients(blocks - 1, 1)
    local_gradients(blocks - 1, 2)
    for q in reversed(range(chips)):

        @pl.when(q > chip)
        def _():
            remote(message, later.at[q], chip_send.at[q], chip_recv.at[q], ctx=sibling).wait_recv()
            for j in range(half):
                half_in[j] = later[q, j, :STATE] + later[q, j, STATE : STATE + 1] * half_in[j]

    hand_over = remote(half_in, sib_half, swap_sem.at[2], swap_sem.at[3], ctx=sibling)
    hand_over.start()
    local_gradients(blocks - 1, 3)
    send_out(blocks - 1)
    hand_over.wait_recv()
    for j in range(half):
        for h, total in ((core * half + j, half_in[j]), ((1 - core) * half + j, sib_half[j])):
            nearer = sib_part[h, :STATE] + sib_part[h, STATE : STATE + 1] * total
            in_ref[h] = jnp.where(core == 1, total, nearer)

    def own_sent(c):
        pl.when(has_left)(lambda: own_copy(c, 0).wait_send())
        pl.when(has_right)(lambda: own_copy(c, 1).wait_send())

    each(count, own_sent)
    if paired:

        @pl.when(inner)
        def _():
            for q in range(chips):
                pl.when(q != chip)(lambda q=q: piece_peer(q).wait_send())
                piece_pair(q).wait_send()

            def passed(c):
                relay(end, c, mate).wait_send()
                sum_copy(c).wait_send()

            each(count, passed)

        pl.when(outer)(lambda: piece_down().wait_send())
    else:
        for d in range(1, tp):

            def passed(c):
                pl.when(jnp.logical_and(z >= d, has_right))(lambda: relay(z - d, c, z + 1).wait_send())
                pl.when(jnp.logical_and(z + d < tp, has_left))(lambda: relay(z + d, c, z - 1).wait_send())

            each(count, passed)
    swap.wait_send()
    for q in range(chips):
        pl.when(q < chip)(lambda q=q: chip_copy(q).wait_send())
    hand_over.wait_send()
    term_copy.wait()
    for b in range(blocks):
        for copy in out_copies(b):
            copy.wait()


def projected(upstream, out_weight, inner_act, head_bc, log_decay, states, skip):
    tp, ctx = lax.axis_size("tp"), lax.axis_size("ctx")
    tokens, depth = upstream.shape
    heads = log_decay.shape[0]
    width, chips, count = heads * HEAD_DIM, ctx // 2, tokens // CHUNK
    paired = tp == 4
    dma = pltpu.SemaphoreType.DMA
    anywhere = pl.BlockSpec(memory_space=pl.ANY)
    vmem = pl.BlockSpec(memory_space=pltpu.VMEM)
    packed = STATE + 8
    sums = (tokens, width) if paired else (16, 128)
    return pl.pallas_call(
        functools.partial(project_kernel, tp, ctx),
        out_shape=(
            jax.ShapeDtypeStruct((tokens, width), F32),
            jax.ShapeDtypeStruct((tokens, width), F32),
            jax.ShapeDtypeStruct(states.shape, F32),
            jax.ShapeDtypeStruct((heads, STATE, HEAD_DIM), F32),
        ),
        in_specs=[
            anywhere,
            anywhere,
            anywhere,
            vmem,
            anywhere,
            anywhere,
            pl.BlockSpec(memory_space=pltpu.SMEM),
        ],
        out_specs=(anywhere, anywhere, anywhere, vmem),
        scratch_shapes=[
            pltpu.VMEM((tp, tokens, depth), BF16),
            pltpu.VMEM(out_weight.shape, BF16),
            pltpu.VMEM(head_bc.shape, BF16),
            pltpu.VMEM((width, 2 * depth) if paired else (16, 128), BF16),
            pltpu.VMEM((tokens, width), F32),
            pltpu.VMEM((BLOCK, width) if paired else (8, 128), F32),
            pltpu.VMEM(sums, BF16),
            pltpu.VMEM(sums, BF16),
            pltpu.VMEM((heads * STATE, tokens), BF16),
            pltpu.VMEM((tokens, width), BF16),
            pltpu.VMEM(states.shape, F32),
            pltpu.VMEM((tokens, width), BF16),
            pltpu.VMEM((tokens, width), F32),
            pltpu.VMEM((tokens, width), F32),
            pltpu.VMEM(states.shape, F32),
            pltpu.VMEM((heads, tokens), F32),
            pltpu.VMEM((tokens, heads), F32),
            pltpu.VMEM((heads, packed, HEAD_DIM), F32),
            pltpu.VMEM((heads, packed, HEAD_DIM), F32),
            pltpu.VMEM((heads // 2, packed, HEAD_DIM), F32),
            pltpu.VMEM((chips, heads // 2, packed, HEAD_DIM), F32),
            pltpu.VMEM((heads // 2, STATE, HEAD_DIM), F32),
            pltpu.VMEM((heads // 2, STATE, HEAD_DIM), F32),
            dma((6,)),
            dma((2, count)),
            dma((tp, count)),
            dma((tp, count)),
            dma((count,)),
            dma((count,)),
            dma,
            dma((chips,)),
            dma((chips,)),
            dma((ctx,)),
            dma((4,)),
            dma((chips,)),
            dma((chips,)),
            dma((2, tokens // BLOCK)),
        ],
        compiler_params=pltpu.CompilerParams(
            collective_id=0, has_side_effects=True, vmem_limit_bytes=56 * 1024 * 1024
        ),
        name="project_and_exchange",
    )(upstream, out_weight, head_bc, log_decay, inner_act, states, skip)


def closing_kernel(
    heads, x_ref, bc_ref, gx0_ref, gbc0_ref, log_ref, s_ref, term_ref, in_ref, gx_ref, gbc_ref, glog_ref, h_ref
):
    @pl.when(pl.program_id(0) == 0)
    def _():
        h_ref[...] = in_ref[...]

    rows, cols = cumulative(log_ref[...])
    last = cols[BLOCK - 1 : BLOCK, :]
    whole, tail = jnp.exp(last), jnp.exp(last - cols)
    sign = jnp.where(lax.broadcasted_iota(jnp.int32, (1, 128), 1) < STATE, -1.0, 1.0)
    lane = lax.broadcasted_iota(jnp.int32, (BLOCK, heads), 1)
    token = lax.broadcasted_iota(jnp.int32, (BLOCK, 1), 0)
    dcum = jnp.zeros((BLOCK, heads), F32)
    for h in range(heads):
        here = slice(h * 128, (h + 1) * 128)
        bc = bc_ref[:, here]
        carried = h_ref[h]
        held = jnp.concatenate([carried, jnp.zeros_like(carried)], axis=0).astype(BF16)
        tail_h, whole_h = tail[:, h : h + 1], whole[:, h : h + 1]
        added = jnp.dot(bc, held, preferred_element_type=F32)
        gx_ref[:, here] = (gx0_ref[:, here] + tail_h * added).astype(BF16)
        wide_tail = tail_h * lax.dot_general(x_ref[:, here], held, LANES, preferred_element_type=F32)
        gbc = gbc0_ref[:, here] + wide_tail
        gbc_ref[:, here] = gbc
        bc_wide = bc.astype(F32)
        dcum_h = jnp.sum(bc_wide * gbc * sign, axis=1, keepdims=True)
        at_end = whole_h * jnp.sum(s_ref[0, h] * carried) + jnp.sum(bc_wide * wide_tail)
        dcum_h = dcum_h + jnp.where(token == BLOCK - 1, at_end, 0.0)
        dcum = jnp.where(lane == h, dcum_h, dcum)
        h_ref[h] = whole_h * carried + term_ref[0, h]
    s_ids = lax.broadcasted_iota(jnp.int32, (BLOCK, BLOCK), 0)
    t_ids = lax.broadcasted_iota(jnp.int32, (BLOCK, BLOCK), 1)
    from_here = jnp.where(s_ids >= t_ids, 1.0, 0.0)
    glog_ref[...] = jnp.dot(
        dcum.T, from_here, precision=lax.Precision.HIGHEST, preferred_element_type=F32
    )


def per_device(upstream, out_weight, inner_act, head_bc, log_decay, states, skip):
    tokens, heads = inner_act.shape[0], log_decay.shape[0]
    width = heads * HEAD_DIM
    blocks = tokens // BLOCK
    gx, gbc, terms, incoming = projected(
        upstream, out_weight, inner_act, head_bc, log_decay, states, skip
    )
    wide = pl.BlockSpec((BLOCK, width), lambda i: (blocks - 1 - i, 0))
    logs = pl.BlockSpec((heads, BLOCK), lambda i: (0, blocks - 1 - i))
    block = pl.BlockSpec((1, heads, STATE, HEAD_DIM), lambda i: (blocks - 1 - i, 0, 0, 0))
    carry = pl.BlockSpec((heads, STATE, HEAD_DIM), lambda i: (0, 0, 0))
    params = pltpu.CompilerParams(
        dimension_semantics=("arbitrary",), vmem_limit_bytes=60 * 1024 * 1024
    )
    return pl.pallas_call(
        functools.partial(closing_kernel, heads),
        out_shape=(
            jax.ShapeDtypeStruct((tokens, width), BF16),
            jax.ShapeDtypeStruct((tokens, width), F32),
            jax.ShapeDtypeStruct((heads, tokens), F32),
        ),
        grid=(blocks,),
        in_specs=[
            wide,
            wide,
            wide,
            wide,
            logs,
            block,
            block,
            carry,
        ],
        out_specs=(wide, wide, logs),
        scratch_shapes=[pltpu.VMEM((heads, STATE, HEAD_DIM), F32)],
        compiler_params=params,
        name="carried_terms",
    )(inner_act, head_bc, gx, gbc, log_decay, states, terms, incoming)


def solution(mesh):
    return jax.shard_map(
        per_device,
        mesh=mesh,
        in_specs=(
            P("ctx", "tp"),
            P("tp", None),
            P("ctx", "tp"),
            P("ctx", "tp"),
            P("tp", "ctx"),
            P("ctx", "tp", None, None),
            P("tp"),
        ),
        out_specs=(P("ctx", "tp"), P("ctx", "tp"), P("tp", "ctx")),
        check_vma=False,
    )
```

```python
import functools

import jax
import jax.numpy as jnp
from jax import lax
from jax.experimental import pallas as pl
from jax.experimental.pallas import tpu as pltpu
from jax.sharding import PartitionSpec as P

HEAD_DIM = 128
STATE = 64
BLOCK = 256
CHUNK = 64
PER = BLOCK // CHUNK
F32 = jnp.float32
BF16 = jnp.bfloat16
ROWS = (((0,), (0,)), ((), ()))
LANES = (((1,), (1,)), ((), ()))


def cumulative(log_rows):
    earlier = lax.broadcasted_iota(jnp.int32, (BLOCK, BLOCK), 0)
    later = lax.broadcasted_iota(jnp.int32, (BLOCK, BLOCK), 1)
    upto = jnp.where(earlier <= later, 1.0, 0.0)
    rows = jnp.dot(log_rows, upto, precision=lax.Precision.HIGHEST, preferred_element_type=F32)
    return rows, rows.T


def part_combined(first, second):
    first_decay = first[STATE : STATE + 1]
    terms = first[:STATE] + first_decay * second[:STATE]
    return jnp.concatenate([terms, first[STATE:] * second[STATE:]], axis=0)


def project_kernel(
    tp,
    ctx,
    up_hbm,
    w_hbm,
    bc_hbm,
    log_ref,
    x_hbm,
    s_hbm,
    skip_ref,
    gx_hbm,
    gbc_hbm,
    term_hbm,
    in_ref,
    got,
    w_ref,
    bc_ref,
    far_w,
    acc,
    mate_sum,
    sum_out,
    sum_in,
    weighted,
    x_ref,
    s_ref,
    dy_ref,
    gx_ref,
    gbc_ref,
    term_ref,
    cum_rows,
    cum_cols,
    part,
    sib_part,
    message,
    later,
    half_in,
    sib_half,
    local_sem,
    own_sem,
    relay_sem,
    got_sem,
    sum_send,
    sum_recv,
    piece_sem,
    peer_sem,
    pair_sem,
    far_sem,
    swap_sem,
    chip_send,
    chip_recv,
    out_sem,
):
    z, me = lax.axis_index("tp"), lax.axis_index("ctx")
    core, chip = lax.rem(me, 2), lax.div(me, 2)
    sibling = me + 1 - 2 * core
    chips = ctx // 2
    heads = log_ref.shape[0]
    half = heads // 2
    tokens, depth = up_hbm.shape
    width = w_hbm.shape[0]
    piece = width // ctx
    count = tokens // CHUNK
    blocks = tokens // BLOCK
    paired = tp == 4
    has_left, has_right = z > 0, z < tp - 1
    inner = jnp.logical_and(has_left, has_right)
    outer = jnp.logical_not(inner)
    low = jnp.where(z <= 1, 2, 0)

    def rows_of(c):
        return pl.ds(pl.multiple_of(c * CHUNK, CHUNK), CHUNK)

    def remote(src, dst, send, recv, **place):
        return pltpu.make_async_remote_copy(
            src_ref=src,
            dst_ref=dst,
            send_sem=send,
            recv_sem=recv,
            device_id=place,
            device_id_type=pl.DeviceIdType.MESH,
        )

    def own_copy(c, side):
        target = z - 1 if side == 0 else z + 1
        return remote(
            up_hbm.at[rows_of(c)], got.at[z, rows_of(c)], own_sem.at[side, c], got_sem.at[z, c], tp=target
        )

    def relay(s, c, target):
        place = got.at[s, rows_of(c)]
        return remote(place, place, relay_sem.at[s, c], got_sem.at[s, c], tp=target)

    def each(n, body):
        lax.fori_loop(0, n, lambda c, unused: (body(c), unused)[1], 0)

    def rows_of_block(b):
        return pl.ds(pl.multiple_of(b * BLOCK, BLOCK), BLOCK)

    def term(s, rows):
        columns = pl.ds(pl.multiple_of(s * depth, depth), depth)
        return lax.dot_general(got[s, rows], w_ref[:, columns], LANES, preferred_element_type=F32)

    def outward(s, rows):
        columns = pl.ds(pl.multiple_of((s - low) * depth, depth), depth)
        return lax.dot_general(got[s, rows], far_w[:, columns], LANES, preferred_element_type=F32)

    def add_term(s, b):
        acc[rows_of_block(b)] += term(s, rows_of_block(b))

    load_w = pltpu.make_async_copy(w_hbm, w_ref, local_sem.at[0])
    load_up = pltpu.make_async_copy(up_hbm, got.at[z], local_sem.at[1])
    load_bc = pltpu.make_async_copy(bc_hbm, bc_ref, local_sem.at[2])
    load_up.start()
    load_w.start()
    load_bc.start()
    load_x = pltpu.make_async_copy(x_hbm, x_ref, local_sem.at[3])
    load_s = pltpu.make_async_copy(s_hbm, s_ref, local_sem.at[4])
    load_x.start()
    load_s.start()

    barrier = pltpu.get_barrier_semaphore()

    def greet(**place):
        pl.semaphore_signal(barrier, inc=1, device_id=place, device_id_type=pl.DeviceIdType.MESH)

    pl.when(has_left)(lambda: greet(tp=z - 1))
    pl.when(has_right)(lambda: greet(tp=z + 1))
    greet(ctx=sibling)
    for q in range(chips):
        pl.when(q != chip)(functools.partial(greet, ctx=2 * q + core))
    pl.semaphore_wait(barrier, chips + has_left.astype(jnp.int32) + has_right.astype(jnp.int32))


    def piece_place(j):
        return far_w.at[pl.ds(pl.multiple_of(j * piece, piece), piece)]

    def piece_down():
        source = w_hbm.at[
            pl.ds(pl.multiple_of(me * piece, piece), piece),
            pl.ds(pl.multiple_of(low * depth, depth), 2 * depth),
        ]
        return remote(source, piece_place(me), piece_sem, far_sem.at[me], tp=jnp.where(z == 0, 1, tp - 2))

    def piece_peer(q):
        place = piece_place(me)
        return remote(place, place, peer_sem.at[q], far_sem.at[me], ctx=2 * q + core)

    def piece_pair(q):
        place = piece_place(2 * q + core)
        return remote(place, place, pair_sem.at[q], far_sem.at[2 * q + core], ctx=sibling)

    def piece_wait(j):
        remote(piece_place(j), piece_place(j), piece_sem, far_sem.at[j], ctx=sibling).wait_recv()

    if paired:
        pl.when(outer)(lambda: piece_down().start())

    def send_own(c):
        early = jnp.logical_or(c < count // 2, not paired)
        pl.when(jnp.logical_and(has_left, jnp.logical_or(early, z != 2)))(lambda: own_copy(c, 0).start())
        pl.when(jnp.logical_and(has_right, jnp.logical_or(early, z != 1)))(lambda: own_copy(c, 1).start())

    each(count, send_own)
    load_up.wait()
    load_w.wait()

    def own_term(b):
        acc[rows_of_block(b)] = term(z, rows_of_block(b))

    each(blocks, own_term)

    if paired:

        @pl.when(inner)
        def _():
            piece_wait(me)
            for q in range(chips):
                pl.when(q != chip)(lambda q=q: piece_peer(q).start())
            piece_pair(chip).start()

    load_bc.wait()

    def weigh(b):
        here = rows_of_block(b)
        rows, cols = cumulative(log_ref[:, here])
        cum_rows[:, here] = rows
        cum_cols[here] = cols
        decay = jnp.exp(rows)
        for h in range(heads):
            c_rows = bc_ref[here, h * 128 : (h + 1) * 128].astype(F32).T[STATE:]
            weighted[h * STATE : (h + 1) * STATE, here] = (c_rows * decay[h : h + 1]).astype(BF16)

    each(blocks, weigh)
    load_x.wait()
    load_s.wait()

    def block_terms(b):
        here = rows_of_block(b)
        for h in range(heads):
            term_ref[b, h] = jnp.dot(
                weighted[h * STATE : (h + 1) * STATE, here],
                dy_ref[here, h * 128 : (h + 1) * 128],
                preferred_element_type=F32,
            )

    k_ids = lax.broadcasted_iota(jnp.int32, (BLOCK, BLOCK), 0)
    q_ids = lax.broadcasted_iota(jnp.int32, (BLOCK, BLOCK), 1)

    def local_gradients(b, group):
        here = rows_of_block(b)
        for h in range(group * heads // PER, (group + 1) * heads // PER):
            at = slice(h * 128, (h + 1) * 128)
            bc, x, dy = bc_ref[here, at], x_ref[here, at], dy_ref[here, at]
            b_rows, c_rows = bc[:, :STATE], bc[:, STATE:]
            column = cum_cols[here, h : h + 1]
            gap = cum_rows[h : h + 1, here] - column
            gate = jnp.exp(jnp.where(q_ids >= k_ids, gap, -1e30))
            scores = lax.dot_general(b_rows, c_rows, LANES, preferred_element_type=F32) * gate
            inside = lax.dot_general(x, dy, LANES, preferred_element_type=F32) * gate
            scores, inside = scores.astype(BF16), inside.astype(BF16)
            gx = jnp.dot(scores, dy, preferred_element_type=F32)
            gx_ref[here, at] = gx + skip_ref[h] * dy.astype(F32)
            gb = jnp.dot(inside, c_rows, preferred_element_type=F32)
            gc = lax.dot_general(inside, b_rows, ROWS, preferred_element_type=F32)
            start = s_ref[b, h].astype(BF16)
            gc += jnp.exp(column) * lax.dot_general(dy, start, LANES, preferred_element_type=F32)
            gbc_ref[here, at] = jnp.concatenate([gb, gc], axis=1)

    def out_copies(b):
        here = rows_of_block(b)
        return (
            pltpu.make_async_copy(gx_ref.at[here], gx_hbm.at[here], out_sem.at[0, b]),
            pltpu.make_async_copy(gbc_ref.at[here], gbc_hbm.at[here], out_sem.at[1, b]),
        )

    def send_out(b):
        for copy in out_copies(b):
            copy.start()

    def drain(arrive, before=None, after=None):
        def take(b):
            if before is not None:
                before(b)
            for i in range(PER):
                dy_ref[rows_of(b * PER + i)] = arrive(b, b * PER + i).astype(BF16)
                pl.when(b > 0)(functools.partial(local_gradients, b - 1, i))
            pl.when(b > 0)(lambda: send_out(b - 1))
            block_terms(b)
            if after is not None:
                after(b)

        each(blocks, take)

    if paired:
        end = jnp.where(z == 1, 0, 3)
        mate, far = 3 - z, 3 - end
        next_in = jnp.where(z == 0, 1, tp - 2)

        def sum_copy(c):
            return remote(
                sum_out.at[rows_of(c)], sum_in.at[rows_of(c)], sum_send.at[c], sum_recv.at[c], tp=end
            )

        def first_hop(c):
            relay(end, c, mate).wait_recv()
            relay(end, c, mate).start()

            @pl.when(c < count - count // 2)
            def _():
                pl.when(z == 2)(lambda: own_copy(c + count // 2, 0).start())
                pl.when(z == 1)(lambda: own_copy(c + count // 2, 1).start())

        first_blocks = (blocks + 1) // 2

        def first_block(b):
            for i in range(PER):
                first_hop(b * PER + i)
            add_term(end, b)

        def mate_block(b):
            for i in range(PER):
                relay(mate, b * PER + i, mate).wait_recv()
            add_term(mate, b)
            mate_sum[...] = outward(mate, rows_of_block(b))

        def second_hop(b, c):
            pl.when(b < blocks - first_blocks)(lambda: first_hop(c + first_blocks * PER))
            relay(far, c, mate).wait_recv()
            in_block = pl.ds(pl.multiple_of((c - b * PER) * CHUNK, CHUNK), CHUNK)
            sum_out[rows_of(c)] = (mate_sum[in_block] + outward(far, rows_of(c))).astype(BF16)
            sum_copy(c).start()
            return acc[rows_of(c)] + term(far, rows_of(c))

        def late_block(b):
            pl.when(b < blocks - first_blocks)(lambda: add_term(end, b + first_blocks))

        @pl.when(inner)
        def _():
            each(first_blocks, first_block)
            for q in range(chips):

                @pl.when(q != chip)
                def _():
                    piece_wait(2 * q + core)
                    piece_pair(q).start()

            for q in range(chips):
                piece_wait(2 * q + 1 - core)
            drain(second_hop, mate_block, late_block)

        def one_hop(b):
            for i in range(PER):
                relay(next_in, b * PER + i, next_in).wait_recv()
            add_term(next_in, b)

        def last_sum(b, c):
            sum_copy(c).wait_recv()
            return acc[rows_of(c)] + sum_in[rows_of(c)].astype(F32)

        @pl.when(outer)
        def _():
            each(blocks, one_hop)
            drain(last_sum)

    else:
        for d in range(1, tp):

            def hop(c):
                @pl.when(z >= d)
                def _():
                    relay(z - d, c, z + 1).wait_recv()
                    pl.when(has_right)(lambda: relay(z - d, c, z + 1).start())
                    acc[rows_of(c)] += term(z - d, rows_of(c))

                @pl.when(z + d < tp)
                def _():
                    relay(z + d, c, z - 1).wait_recv()
                    pl.when(has_left)(lambda: relay(z + d, c, z - 1).start())
                    acc[rows_of(c)] += term(z + d, rows_of(c))

            each(count, hop)
        drain(lambda b, c: acc[rows_of(c)])

    for h in range(heads):
        total, decay = term_ref[blocks - 1, h], 0.0
        for b in reversed(range(blocks)):
            log = cum_rows[h : h + 1, (b + 1) * BLOCK - 1 : (b + 1) * BLOCK]
            decay = decay + log
            if b < blocks - 1:
                total = term_ref[b, h] + jnp.exp(log) * total
        part[h, :STATE] = total
        part[h, STATE:] = jnp.broadcast_to(jnp.exp(decay), (8, HEAD_DIM))
    term_copy = pltpu.make_async_copy(term_ref, term_hbm, local_sem.at[5])
    term_copy.start()

    swap = remote(part, sib_part, swap_sem.at[0], swap_sem.at[1], ctx=sibling)
    swap.start()
    local_gradients(blocks - 1, 0)
    swap.wait_recv()
    for j in range(half):
        mine, other = part[core * half + j], sib_part[core * half + j]
        first, second = jnp.where(core == 0, mine, other), jnp.where(core == 0, other, mine)
        message[j] = part_combined(first, second)

    def chip_copy(q):
        return remote(message, later.at[chip], chip_send.at[q], chip_recv.at[chip], ctx=2 * q + core)

    for q in reversed(range(chips)):
        pl.when(q < chip)(lambda q=q: chip_copy(q).start())
    half_in[...] = jnp.zeros_like(half_in)
    local_gradients(blocks - 1, 1)
    local_gradients(blocks - 1, 2)
    for q in reversed(range(chips)):

        @pl.when(q > chip)
        def _():
            remote(message, later.at[q], chip_send.at[q], chip_recv.at[q], ctx=sibling).wait_recv()
            for j in range(half):
                half_in[j] = later[q, j, :STATE] + later[q, j, STATE : STATE + 1] * half_in[j]

    hand_over = remote(half_in, sib_half, swap_sem.at[2], swap_sem.at[3], ctx=sibling)
    hand_over.start()
    local_gradients(blocks - 1, 3)
    send_out(blocks - 1)
    hand_over.wait_recv()
    for j in range(half):
        for h, total in ((core * half + j, half_in[j]), ((1 - core) * half + j, sib_half[j])):
            nearer = sib_part[h, :STATE] + sib_part[h, STATE : STATE + 1] * total
            in_ref[h] = jnp.where(core == 1, total, nearer)

    def own_sent(c):
        pl.when(has_left)(lambda: own_copy(c, 0).wait_send())
        pl.when(has_right)(lambda: own_copy(c, 1).wait_send())

    each(count, own_sent)
    if paired:

        @pl.when(inner)
        def _():
            for q in range(chips):
                pl.when(q != chip)(lambda q=q: piece_peer(q).wait_send())
                piece_pair(q).wait_send()

            def passed(c):
                relay(end, c, mate).wait_send()
                sum_copy(c).wait_send()

            each(count, passed)

        pl.when(outer)(lambda: piece_down().wait_send())
    else:
        for d in range(1, tp):

            def passed(c):
                pl.when(jnp.logical_and(z >= d, has_right))(lambda: relay(z - d, c, z + 1).wait_send())
                pl.when(jnp.logical_and(z + d < tp, has_left))(lambda: relay(z + d, c, z - 1).wait_send())

            each(count, passed)
    swap.wait_send()
    for q in range(chips):
        pl.when(q < chip)(lambda q=q: chip_copy(q).wait_send())
    hand_over.wait_send()
    term_copy.wait()
    for b in range(blocks):
        for copy in out_copies(b):
            copy.wait()


def projected(upstream, out_weight, inner_act, head_bc, log_decay, states, skip):
    tp, ctx = lax.axis_size("tp"), lax.axis_size("ctx")
    tokens, depth = upstream.shape
    heads = log_decay.shape[0]
    width, chips, count = heads * HEAD_DIM, ctx // 2, tokens // CHUNK
    paired = tp == 4
    dma = pltpu.SemaphoreType.DMA
    anywhere = pl.BlockSpec(memory_space=pl.ANY)
    vmem = pl.BlockSpec(memory_space=pltpu.VMEM)
    packed = STATE + 8
    sums = (tokens, width) if paired else (16, 128)
    return pl.pallas_call(
        functools.partial(project_kernel, tp, ctx),
        out_shape=(
            jax.ShapeDtypeStruct((tokens, width), F32),
            jax.ShapeDtypeStruct((tokens, width), F32),
            jax.ShapeDtypeStruct(states.shape, F32),
            jax.ShapeDtypeStruct((heads, STATE, HEAD_DIM), F32),
        ),
        in_specs=[
            anywhere,
            anywhere,
            anywhere,
            vmem,
            anywhere,
            anywhere,
            pl.BlockSpec(memory_space=pltpu.SMEM),
        ],
        out_specs=(anywhere, anywhere, anywhere, vmem),
        scratch_shapes=[
            pltpu.VMEM((tp, tokens, depth), BF16),
            pltpu.VMEM(out_weight.shape, BF16),
            pltpu.VMEM(head_bc.shape, BF16),
            pltpu.VMEM((width, 2 * depth) if paired else (16, 128), BF16),
            pltpu.VMEM((tokens, width), F32),
            pltpu.VMEM((BLOCK, width) if paired else (8, 128), F32),
            pltpu.VMEM(sums, BF16),
            pltpu.VMEM(sums, BF16),
            pltpu.VMEM((heads * STATE, tokens), BF16),
            pltpu.VMEM((tokens, width), BF16),
            pltpu.VMEM(states.shape, F32),
            pltpu.VMEM((tokens, width), BF16),
            pltpu.VMEM((tokens, width), F32),
            pltpu.VMEM((tokens, width), F32),
            pltpu.VMEM(states.shape, F32),
            pltpu.VMEM((heads, tokens), F32),
            pltpu.VMEM((tokens, heads), F32),
            pltpu.VMEM((heads, packed, HEAD_DIM), F32),
            pltpu.VMEM((heads, packed, HEAD_DIM), F32),
            pltpu.VMEM((heads // 2, packed, HEAD_DIM), F32),
            pltpu.VMEM((chips, heads // 2, packed, HEAD_DIM), F32),
            pltpu.VMEM((heads // 2, STATE, HEAD_DIM), F32),
            pltpu.VMEM((heads // 2, STATE, HEAD_DIM), F32),
            dma((6,)),
            dma((2, count)),
            dma((tp, count)),
            dma((tp, count)),
            dma((count,)),
            dma((count,)),
            dma,
            dma((chips,)),
            dma((chips,)),
            dma((ctx,)),
            dma((4,)),
            dma((chips,)),
            dma((chips,)),
            dma((2, tokens // BLOCK)),
        ],
        compiler_params=pltpu.CompilerParams(
            collective_id=0, has_side_effects=True, vmem_limit_bytes=56 * 1024 * 1024
        ),
        name="project_and_exchange",
    )(upstream, out_weight, head_bc, log_decay, inner_act, states, skip)


def closing_kernel(
    heads, x_ref, bc_ref, gx0_ref, gbc0_ref, log_ref, s_ref, term_ref, in_ref, gx_ref, gbc_ref, glog_ref, h_ref
):
    @pl.when(pl.program_id(0) == 0)
    def _():
        h_ref[...] = in_ref[...]

    rows, cols = cumulative(log_ref[...])
    last = cols[BLOCK - 1 : BLOCK, :]
    whole, tail = jnp.exp(last), jnp.exp(last - cols)
    sign = jnp.where(lax.broadcasted_iota(jnp.int32, (1, 128), 1) < STATE, -1.0, 1.0)
    lane = lax.broadcasted_iota(jnp.int32, (BLOCK, heads), 1)
    at_end = []
    dcum = jnp.zeros((BLOCK, heads), F32)
    for h in range(heads):
        here = slice(h * 128, (h + 1) * 128)
        bc = bc_ref[:, here]
        carried = h_ref[h]
        held = jnp.concatenate([carried, jnp.zeros_like(carried)], axis=0).astype(BF16)
        tail_h, whole_h = tail[:, h : h + 1], whole[:, h : h + 1]
        added = jnp.dot(bc, held, preferred_element_type=F32)
        gx_ref[:, here] = (gx0_ref[:, here] + tail_h * added).astype(BF16)
        wide_tail = tail_h * lax.dot_general(x_ref[:, here], held, LANES, preferred_element_type=F32)
        gbc = gbc0_ref[:, here] + wide_tail
        gbc_ref[:, here] = gbc
        bc_wide = bc.astype(F32)
        dcum_h = jnp.sum(bc_wide * gbc * sign, axis=1, keepdims=True)
        of_start = jnp.sum(s_ref[0, h] * carried, axis=0, keepdims=True)
        at_end.append(whole_h * of_start + jnp.sum(bc_wide * wide_tail, axis=0, keepdims=True))
        dcum = jnp.where(lane == h, dcum_h, dcum)
        h_ref[h] = whole_h * carried + term_ref[0, h]
    s_ids = lax.broadcasted_iota(jnp.int32, (BLOCK, BLOCK), 0)
    t_ids = lax.broadcasted_iota(jnp.int32, (BLOCK, BLOCK), 1)
    from_here = jnp.where(s_ids >= t_ids, 1.0, 0.0)
    glog = jnp.dot(dcum.T, from_here, precision=lax.Precision.HIGHEST, preferred_element_type=F32)
    glog_ref[...] = glog + jnp.sum(jnp.concatenate(at_end, axis=0), axis=1, keepdims=True)


def per_device(upstream, out_weight, inner_act, head_bc, log_decay, states, skip):
    tokens, heads = inner_act.shape[0], log_decay.shape[0]
    width = heads * HEAD_DIM
    blocks = tokens // BLOCK
    gx, gbc, terms, incoming = projected(
        upstream, out_weight, inner_act, head_bc, log_decay, states, skip
    )
    wide = pl.BlockSpec((BLOCK, width), lambda i: (blocks - 1 - i, 0))
    logs = pl.BlockSpec((heads, BLOCK), lambda i: (0, blocks - 1 - i))
    block = pl.BlockSpec((1, heads, STATE, HEAD_DIM), lambda i: (blocks - 1 - i, 0, 0, 0))
    carry = pl.BlockSpec((heads, STATE, HEAD_DIM), lambda i: (0, 0, 0))
    params = pltpu.CompilerParams(
        dimension_semantics=("arbitrary",), vmem_limit_bytes=60 * 1024 * 1024
    )
    return pl.pallas_call(
        functools.partial(closing_kernel, heads),
        out_shape=(
            jax.ShapeDtypeStruct((tokens, width), BF16),
            jax.ShapeDtypeStruct((tokens, width), F32),
            jax.ShapeDtypeStruct((heads, tokens), F32),
        ),
        grid=(blocks,),
        in_specs=[
            wide,
            wide,
            wide,
            wide,
            logs,
            block,
            block,
            carry,
        ],
        out_specs=(wide, wide, logs),
        scratch_shapes=[pltpu.VMEM((heads, STATE, HEAD_DIM), F32)],
        compiler_params=params,
        name="carried_terms",
    )(inner_act, head_bc, gx, gbc, log_decay, states, terms, incoming)


def solution(mesh):
    return jax.shard_map(
        per_device,
        mesh=mesh,
        in_specs=(
            P("ctx", "tp"),
            P("tp", None),
            P("ctx", "tp"),
            P("ctx", "tp"),
            P("tp", "ctx"),
            P("ctx", "tp", None, None),
            P("tp"),
        ),
        out_specs=(P("ctx", "tp"), P("ctx", "tp"), P("tp", "ctx")),
        check_vma=False,
    )
```
